128 devices in a mesh: gx: 2 (over core), gy: 32 (over z, y, x_hi), gz: 2 (over x_lo).
Axes of the slice: x: 4 (x_hi: 2, x_lo: 2; x = x_hi * 2 + x_lo), y: 4, z: 4, core: 2. Of those that a mesh axis runs over, the one named last changes fastest.
Arguments:
- coords: float32 [3, 8, 8, 128, 32], P(None, None, 'gx', 'gy', 'gz'), may hold values from -0.5 to 0.5
- velocity: float32 [3, 8, 8, 128, 32], P(None, None, 'gx', 'gy', 'gz'), may hold values from -3 to 3
- bead_type: int32 [8, 8, 128, 32], P(None, 'gx', 'gy', 'gz'), may hold values from 0 to 15
- eps_table: float32 [16, 16], replicated, may hold values from 0.2 to 2
- pair_list: int32 [14, 8, 128, 32], P(None, 'gx', 'gy', 'gz'), may hold values 0 or 1
- migration: int32 [2, 4, 2], replicated, may hold values from 0 to 15, as said below
Outputs:
- positions: float32 [3, 8, 8, 128, 32], P(None, None, 'gx', 'gy', 'gz')
- velocities: float32 [3, 8, 8, 128, 32], P(None, None, 'gx', 'gy', 'gz')
The draws below stay inside these ranges and needn't reach their ends.
Inputs may be any that keep to these rules, and one draw needn't show every extreme that they name: `migration`: within each step the 8 listed column numbers are distinct.
All inputs are finite; a program needn't handle non-finite values. No bound on the sum of `pair_list` on one device may be relied on, other than what follows from the above.
Results may differ from the reference program's by a relative error of at most 0.0003.
Values sent between devices are 32-bit elements; how exact they have to be, the bound alone decides.
A program may use at most 128 MiB of HBM per device.

```python
import math
import jax
import jax.numpy as jnp
from jax import lax

NCX = 4
NCY = 4
STEPS = 2
MIGC = 2
NTYPES = 16
NX = 8
NY = 128
NZ = 32
N_GX = 2
N_GY = 32


def draw_migration(key, part):
    key = jax.random.fold_in(key, 5)
    columns = NCX * NCY
    listed = 4 * MIGC
    per_step = []
    for step in range(STEPS):
        step_key = jax.random.fold_in(key, step)
        middle = jax.random.permutation(jax.random.fold_in(step_key, 1), columns - 2) + 1
        picked = jnp.concatenate([jnp.array([0, columns - 1], jnp.int32), middle[:listed - 2].astype(jnp.int32)])
        arrange = jax.random.permutation(jax.random.fold_in(step_key, 2), listed)
        per_step.append(picked[arrange].reshape(4, MIGC))
    return jnp.stack(per_step)


def with_ends(values, own_key, least, largest):
    place = [jax.random.randint(jax.random.fold_in(own_key, axis), (), 0, length) for axis, length in enumerate(values.shape)]
    main_axis = values.shape.index(max(values.shape))
    neighbour = place[:main_axis] + [(place[main_axis] + 1) % values.shape[main_axis]] + place[main_axis + 1:]
    return values.at[tuple(place)].set(least).at[tuple(neighbour)].set(largest)


def level_of(own_key, shape, cuts, least, top_value):
    loudness, own = 1.0, jax.random.fold_in(own_key, 6)
    for position, blocks in cuts:
        draws = jnp.exp(jax.random.uniform(jax.random.fold_in(own, position), (blocks,), jnp.float32, least / len(cuts), top_value / len(cuts)))
        loudness = loudness * jnp.repeat(draws, shape[position] // blocks).reshape([-1 if axis == position else 1 for axis in range(len(shape))])
    return loudness


def gaussian(rng, extent, width, reach, split=(), kind=jnp.bfloat16):
    result = jax.random.normal(rng, extent, jnp.float32) * width
    if len(split) > 0:
        result = level_of(rng, extent, split, -0.22, 0.18) * result
    return jnp.clip(result, min=-reach, max=reach).astype(kind)


def setup_inputs(seed: int = 0) -> dict:
    splits = jax.random.split(jax.random.key(seed), 7)
    return {
        "coords": jnp.clip(jax.random.uniform(splits[0], (3, 8, NX, NY, NZ), jnp.float32, -0.5, 0.5) * level_of(splits[0], (3, 8, NX, NY, NZ), ((2, 2), (3, 32), (4, 2)), -0.4, 0.0), -0.5, 0.5),
        "velocity": gaussian(splits[1], (3, 8, NX, NY, NZ), 0.5, 3.0, ((2, 2), (3, 32), (4, 2)), jnp.float32),
        "bead_type": with_ends(jax.random.randint(splits[2], (8, NX, NY, NZ), 0, NTYPES), jax.random.fold_in(splits[2], 1), 0, NTYPES - 1).astype(jnp.int32),
        "eps_table": jnp.clip(jnp.exp(jax.random.uniform(splits[3], (NTYPES, NTYPES), jnp.float32, math.log(0.2), math.log(2.0))), 0.2, 2.0),
        "pair_list": with_ends((jax.random.randint(splits[4], (14, NX, NY, NZ), 0, 4) < 3).astype(jnp.int32), jax.random.fold_in(splits[4], 1), 0, 1),
        "migration": draw_migration(jax.random.fold_in(splits[6], 71), 0),
    }


step_time = 0.02
soft_core = 0.3
cutoff_sq = 2.25
half_shell = [(a, b, c) for a in (-1, 0, 1) for b in (-1, 0, 1) for c in (-1, 0, 1) if (a, b, c) > (0, 0, 0)]


def pair_force(coords_i, coords_j, rates_i, onehot_j, offset, listed, both):
    high = lax.Precision.HIGHEST
    dist_sq = 0.0
    for axis_k in range(3):
        delta = coords_i[axis_k][:, None] - coords_j[axis_k][None, :] - float(offset[axis_k])
        dist_sq = dist_sq + delta * delta
    strength = jnp.einsum("si...,sj...->ij...", rates_i, onehot_j, precision=high)
    inverse = 1.0 / (dist_sq + soft_core)
    switch = jnp.square(jnp.maximum(1.0 - dist_sq / cutoff_sq, 0.0))
    weight = strength * (inverse ** 4 - inverse ** 2) * switch * listed.astype(jnp.float32)[None, None]
    sum_over_j = weight.sum(1)
    on_first = []
    for axis_k in range(3):
        pulled = jnp.einsum("ij...,j...->i...", weight, coords_j[axis_k], precision=high)
        on_first.append((coords_i[axis_k] - float(offset[axis_k])) * sum_over_j - pulled)
    if not both:
        return jnp.stack(on_first), None
    sum_over_i = weight.sum(0)
    on_second = []
    for axis_k in range(3):
        pushed = jnp.einsum("ij...,i...->j...", weight, coords_i[axis_k], precision=high)
        on_second.append((coords_j[axis_k] + float(offset[axis_k])) * sum_over_i - pushed)
    return jnp.stack(on_first), jnp.stack(on_second)


def total_force(coords, kinds, table, pair_list):
    types = jnp.arange(NTYPES, dtype=jnp.float32).reshape(-1, 1, 1, 1, 1)
    onehot = (kinds[None] == types).astype(jnp.float32)
    rates = jnp.einsum("st,t...->s...", table, onehot, precision=lax.Precision.HIGHEST)
    total, unused = pair_force(coords, coords, rates, onehot, (0, 0, 0), pair_list[0], False)
    axes_last = (-3, -2, -1)
    for index, offset in enumerate(half_shell):
        back = tuple(-value for value in offset)
        near_coords = jnp.roll(coords, back, axis=axes_last)
        near_onehot = jnp.roll(onehot, back, axis=axes_last)
        on_first, on_second = pair_force(coords, near_coords, rates, near_onehot, offset, pair_list[index + 1], True)
        total = total + on_first + jnp.roll(on_second, offset, axis=axes_last)
    return total


def migrate(state, lists):
    count_rows = state.shape[0]
    blocks = state.reshape(count_rows, 8, N_GX, NCX, N_GY, NCY, NZ).transpose(0, 1, 2, 4, 6, 3, 5)
    blocks = blocks.reshape(count_rows, 8, N_GX, N_GY, NZ, NCX * NCY)
    for direction, (axis_dom, amount) in enumerate(((2, 1), (2, -1), (3, 1), (3, -1))):
        chosen = lists[direction]
        moved = jnp.roll(blocks[..., chosen], amount, axis=axis_dom)
        blocks = blocks.at[..., chosen].set(moved)
    blocks = blocks.reshape(count_rows, 8, N_GX, N_GY, NZ, NCX, NCY).transpose(0, 1, 2, 5, 3, 6, 4)
    return blocks.reshape(count_rows, 8, NX, NY, NZ)


def reference(coords, velocity, bead_type, eps_table, pair_list, migration):
    table = 0.5 * (eps_table + eps_table.T)
    state = jnp.concatenate([coords, velocity, bead_type.astype(jnp.float32)[None]], 0)
    for step in range(STEPS):
        state = migrate(state, migration[step])
        coords, velocity, kinds = state[0:3], state[3:6], state[6]
        force = total_force(coords, kinds, table, pair_list)
        velocity = velocity + step_time * force
        coords = coords + step_time * velocity
        state = jnp.concatenate([coords, velocity, kinds[None]], 0)
    return coords, velocity
```

```python
import functools

import jax
import jax.numpy as jnp
from jax import lax
from jax.experimental import pallas as pl
from jax.experimental.pallas import tpu as pltpu
from jax.sharding import PartitionSpec as P

MESH = pl.DeviceIdType.MESH
F32 = jnp.float32
STEPS = 2
STEP_TIME = 0.02
SOFT = 0.3
NEAR = 1.0 / (2.25 + 0.3)
SCALE = ((2.25 + 0.3) / 2.25) ** 2
FAR = 1.0e3
half_shell = [
    (a, b, c) for a in (-1, 0, 1) for b in (-1, 0, 1) for c in (-1, 0, 1) if (a, b, c) > (0, 0, 0)
]
all_shell = [(a, b, c) for a in (-1, 0, 1) for b in (-1, 0, 1) for c in (-1, 0, 1)]


def column_lane(k):
    cx, cy = k // 4, k % 4
    return cy // 2, (cy % 2) * 64 + cx * 16


def roll(x, count):
    return pltpu.roll(x, count % 128, 1)


def perm(x, index):
    return jnp.take_along_axis(x, index, axis=1, mode="promise_in_bounds")


def halves(ref, *lead):
    return [ref[(*lead, slice(None), slice(v * 128, v * 128 + 128))] for v in range(2)]


def kernel(
    coords_hbm, velocity_hbm, type_hbm, eps_ref, pairs_hbm, lists_ref,
    pos_ref, vel_ref,
    raw_c, raw_v, raw_t, raw_p,
    own, par, sy, zo, zy, ry, rz, ryz, r2,
    shell, shell_type, away,
    in_sem, send_sem, recv_sem,
):
    gx, gy, gz = lax.axis_index("gx"), lax.axis_index("gy"), lax.axis_index("gz")
    ring = lax.axis_size("gy")

    def device(tx, dy, tz):
        return (
            1 - gx if tx else gx,
            lax.rem(gy + (dy + ring), ring) if dy else gy,
            1 - gz if tz else gz,
        )

    partners = [
        (tx, dy, tz)
        for dy in (1, -1, 2, -2, 0)
        for tz in (0, 1)
        for tx in (0, 1)
        if (tx, dy, tz) != (0, 0, 0)
    ]
    loads = [
        pltpu.make_async_copy(coords_hbm, raw_c, in_sem.at[0]),
        pltpu.make_async_copy(velocity_hbm, raw_v, in_sem.at[1]),
        pltpu.make_async_copy(type_hbm, raw_t, in_sem.at[2]),
        pltpu.make_async_copy(pairs_hbm, raw_p.at[pl.ds(0, 224)], in_sem.at[3]),
    ]
    for load in loads:
        load.start()
    barrier = pltpu.get_barrier_semaphore()
    for partner in partners:
        pl.semaphore_signal(barrier, inc=1, device_id=device(*partner), device_id_type=MESH)

    lane = lax.broadcasted_iota(jnp.int32, (8, 128), 1)
    z = lane & 15
    group = lane & ~15
    cx = (lane >> 4) & 3
    lower = lane < 64
    swapped = jnp.where(z == 15, 0, 1)
    slot = (lane >> 1) & 7

    tables = []
    tiled = [jnp.concatenate([eps_ref[r : r + 1, :]] * 8, axis=1) for r in range(16)]
    tiled = [jnp.broadcast_to(row, (8, 128)) for row in tiled]
    for h in range(2):
        direct = jnp.zeros((8, 128), F32)
        transposed = jnp.zeros((8, 128), F32)
        for r in range(8):
            direct = jnp.where((lane >> 4) == r, tiled[8 * h + r], direct)
        for c in range(16):
            transposed = jnp.where(z == c, perm(tiled[c], (lane >> 4) + 8 * h), transposed)
        tables.append((0.5 * SCALE) * (direct + transposed))

    raw_p[pl.ds(224, 32), :] = jnp.zeros((32, 16), jnp.int32)
    for load in loads:
        load.wait()
    sources = [(raw_c, 0), (raw_c, 1), (raw_c, 2), (raw_t, 0), (raw_v, 0), (raw_v, 1), (raw_v, 2), (raw_p, 0), (raw_p, 1)]
    for q, (raw, block) in enumerate(sources):
        for v in range(2):
            pieces = []
            for part in range(8):
                k = (part % 4) * 4 + v * 2 + part // 4
                pieces.append(raw[pl.ds(block * 128 + k, 8, stride=16), :])
            own[0, q, :, v * 128 : v * 128 + 128] = jnp.concatenate(pieces, axis=1).astype(F32)

    def pack(s):
        state = [halves(own, s, q) for q in range(9 if s == 0 else 7)]
        for d in range(2):
            v = 1 - d

            def pair(first, second):
                if d == 0:
                    return jnp.where(lower, roll(state[first][v], 64), state[second][v])
                return jnp.where(lower, state[first][v], roll(state[second][v], 64))

            a, b = pair(0, 1), pair(2, 3)
            listed = []
            for rows in ((0, 1, 2, 3), (4, 5, 6)):
                out = jnp.zeros((8, 128), F32)
                for m in range(2):
                    k = lists_ref[s, m, 2 + d]
                    in_second = (k & 3) >= 2
                    start = (k & 1) * 64 + (k >> 2) * 16
                    index = start + z
                    for i, q in enumerate(rows):
                        value = jnp.where(in_second, state[q][1], state[q][0])
                        out = jnp.where((lane >> 4) == 2 * i + m, perm(value, index), out)
                listed.append(out)
            sy[s, d, 1] = listed[0]
            sy[s, d, 2] = a
            sy[s, d, 3] = b
            sy[s, d, 4] = listed[1]
            ends = group + 15 * (lane & 1)
            thin = jnp.zeros((8, 128), F32)
            slots = [a, b, listed[0]]
            if s == 0:
                p = pair(7, 8)
                sy[s, d, 0] = p
                slots.append(p)
            for i, value in enumerate(slots):
                thin = jnp.where(slot == i, perm(value, ends), thin)
            zy[s, d] = thin
        ends = group + 15 * (lane & 1)
        for part, rows in enumerate(((0, 1, 2, 3), (7, 8))[: 2 if s == 0 else 1]):
            thin = jnp.zeros((8, 128), F32)
            for i, q in enumerate(rows):
                for v in range(2):
                    thin = jnp.where(slot == 2 * i + v, perm(state[q][v], ends), thin)
            zo[s, part] = thin

    def send(s):
        first = 0 if s == 0 else 1
        plan = []
        for d, dy in ((0, 1), (1, -1)):
            wide, narrow = pl.ds(first, 5 - first), pl.ds(first, 4 - first)
            plan.append(((0, dy, 0), sy.at[s, d, wide], ry.at[s, 0, d, wide]))
            plan.append(((1, dy, 0), sy.at[s, d, narrow], ry.at[s, 1, d, narrow]))
            for tx in range(2):
                plan.append(((tx, dy, 1), zy.at[s, d], ryz.at[s, tx, d]))
        for d, dy in ((0, 2), (1, -2)):
            for tx in range(2):
                for tz in range(2):
                    plan.append(((tx, dy, tz), sy.at[s, d, 1], r2.at[s, tx, tz, d]))
        parts = pl.ds(0, 2 if s == 0 else 1)
        for tx in range(2):
            plan.append(((tx, 0, 1), zo.at[s, parts], rz.at[s, tx, parts]))
        rows = pl.ds(0, 9 if s == 0 else 7)
        plan.append(((1, 0, 0), own.at[s, rows], par.at[s, rows]))
        copies = []
        for i, (to, src, dst) in enumerate(plan):
            copy = pltpu.make_async_remote_copy(
                src_ref=src,
                dst_ref=dst,
                send_sem=send_sem.at[s, i],
                recv_sem=recv_sem.at[s, i],
                device_id=device(*to),
                device_id_type=MESH,
            )
            copy.start()
            copies.append(copy)
        return copies

    def weave(p0, p1, ym, yp):
        r0, r1 = roll(p0, 64), roll(p1, 64)
        return [jnp.where(lower, ym, r0), p0, jnp.where(lower, r0, r1), p1, jnp.where(lower, r1, yp)]

    def shifts(near):
        out = {}
        for a in (-1, 0, 1):
            along = []
            for dz in range(2):
                mine, other = near[0][dz], near[1][dz]
                if a == 0:
                    along.append(mine)
                else:
                    edge = cx == (3 if a == 1 else 0)
                    along.append([
                        jnp.where(edge, roll(o, 48 * a), roll(m, -16 * a)) for m, o in zip(mine, other)
                    ])
            out[a, 0] = along[0]
            out[a, 1] = [jnp.where(z == 15, o, roll(m, -1)) for m, o in zip(*along)]
            out[a, -1] = [jnp.where(z == 0, o, roll(m, 1)) for m, o in zip(*along)]
        return out

    def of_shell(shifted, offset):
        a, b, c = offset
        five = shifted[a, c]
        return {-1: (five[0], five[2]), 0: (five[1], five[3]), 1: (five[2], five[4])}[b]

    def edge_of(two, q, d):
        return two if q % 2 == d else roll(two, 64)

    def pair_weights():
        power = [jnp.left_shift(1, lax.broadcasted_iota(jnp.int32, (8, 128), 0) + 8 * g).astype(F32) for g in range(2)]

        def bits(first, second):
            total = jnp.sum(first * power[0] + second * power[1], axis=0, keepdims=True)
            return jnp.broadcast_to(total, (8, 128))

        near = []
        for dx in range(2):
            row = []
            src = own.at[0] if dx == 0 else par.at[0]
            for dz in range(2):
                if dz == 0:
                    planes = [halves(src, q) for q in (7, 8)]
                    edges = [ry[0, dx, d, 0] for d in range(2)]
                else:
                    thin = rz[0, dx, 1]
                    planes = [[perm(thin, group + 2 * (2 * g + v) + swapped) for v in range(2)] for g in range(2)]
                    edges = [perm(ryz[0, dx, d], group + 6 + swapped) for d in range(2)]
                p = [bits(planes[0][v], planes[1][v]) for v in range(2)]
                y = [bits(edge_of(edges[d], 0, d), edge_of(edges[d], 1, d)) for d in range(2)]
                row.append(weave(p[0], p[1], y[0], y[1]))
            near.append(row)
        shifted = shifts(near)
        for o, offset in enumerate(all_shell):
            if offset >= (0, 0, 0):
                number = 0 if offset == (0, 0, 0) else 1 + half_shell.index(offset)
                two = of_shell(shifted, (0, 0, 0))
            else:
                number = 1 + half_shell.index(tuple(-value for value in offset))
                two = of_shell(shifted, offset)
            for v in range(2):
                listed = ((two[v].astype(jnp.int32) >> number) & 1) == 1
                away[o, :, v * 128 : v * 128 + 128] = jnp.where(listed, F32(offset[0]), F32(FAR))

    def assemble(s):
        column = [cx * 4 + (lane >> 6), cx * 4 + (lane >> 6) + 2, cx * 4 + 3, cx * 4]
        listed = [[lists_ref[s, m, d] for m in range(2)] for d in range(4)]

        def member(k, names):
            out = k == names[0]
            for name in names[1:]:
                out = out | (k == name)
            return out

        swap = [member(k, listed[0] + listed[1]) for k in column]
        moved = [[member(k, listed[2 + d]) for d in range(2)] for k in column]
        which = [[jnp.where(k == listed[2 + d][1], 16, 0) for d in range(2)] for k in column]
        state = [None] * 7
        for q in range(4):
            near = [[None, None], [None, None]]
            for dz in range(2):
                if dz == 0:
                    plane = [halves(own, s, q), halves(par, s, q)]
                    edge = [[edge_of(ry[s, dx, d, 2 + q // 2], q, d) for d in range(2)] for dx in range(2)]
                    beyond = [[w[d] + (z + 32 * q) for d in range(2)] for w in which]
                    near_list = [[ry[s, dx, d, 1] for d in range(2)] for dx in range(2)]
                    close = beyond
                else:
                    plane = [
                        [perm(rz[s, dx, 0], group + (4 * q + 2 * v) + swapped) for v in range(2)]
                        for dx in range(2)
                    ]
                    near_list = [[ryz[s, dx, d] for d in range(2)] for dx in range(2)]
                    start = [(group & 63) + 64 * (q % 2) + 2 * (q // 2) + swapped for d in range(2)]
                    edge = [[perm(near_list[dx][d], start[d]) for d in range(2)] for dx in range(2)]
                    beyond = [[w[d] + (15 - z + 32 * q) for d in range(2)] for w in which]
                    close = [[w[d] + (32 * q + 4) + swapped for d in range(2)] for w in which]
                far_list = [[r2[s, dx, dz, d] for d in range(2)] for dx in range(2)]
                for dx in range(2):
                    p = []
                    for v in range(2):
                        value = plane[dx][v]
                        for d in range(2):
                            value = jnp.where(moved[v][d], perm(near_list[dx][d], close[v][d]), value)
                        p.append(jnp.where(swap[v], plane[1 - dx][v], value))
                    y = []
                    for d in range(2):
                        i = 2 + d
                        value = edge[dx][d]
                        value = jnp.where(moved[i][d], perm(far_list[dx][d], beyond[i][d]), value)
                        value = jnp.where(moved[i][1 - d], roll(plane[dx][1 - d], 64), value)
                        y.append(jnp.where(swap[i], edge[1 - dx][d], value))
                    near[dx][dz] = weave(p[0], p[1], y[0], y[1])
            state[q] = [near[0][0][1], near[0][0][3]]
            shifted = shifts(near)
            for o, offset in enumerate(all_shell):
                two = of_shell(shifted, offset)
                for v in range(2):
                    at = slice(v * 128, v * 128 + 128)
                    if q == 0:
                        shell[o, 0, :, at] = two[v] + away[o, :, at]
                    elif q < 3:
                        shell[o, q, :, at] = two[v] + F32(offset[q]) if offset[q] else two[v]
                    else:
                        shell_type[o, :, at] = two[v].astype(jnp.int32)
        for q in range(4, 7):
            mine, other = halves(own, s, q), halves(par, s, q)
            state[q] = []
            for v in range(2):
                value = mine[v]
                for d in range(2):
                    value = jnp.where(moved[v][d], perm(ry[s, 0, d, 4], which[v][d] + (z + 32 * (q - 4))), value)
                state[q].append(jnp.where(swap[v], other[v], value))
        return state

    def forces(state):
        kinds = [value.astype(jnp.int32) for value in state[3]]
        base = [(value & 7) * 16 for value in kinds]
        low = [value < 8 for value in kinds]

        def add(o, sums):
            sums = list(sums)
            for v in range(2):
                at = slice(v * 128, v * 128 + 128)
                for j in range(8):
                    d = [state[q][v] - jnp.broadcast_to(shell[o, q, j : j + 1, at], (8, 128)) for q in range(3)]
                    apart = d[0] * d[0] + d[1] * d[1] + (d[2] * d[2] + SOFT)
                    u = pl.reciprocal(apart, approx=True)
                    reach = jnp.maximum(u - NEAR, 0.0)
                    index = base[v] + jnp.broadcast_to(shell_type[o, j : j + 1, at], (8, 128))
                    strength = jnp.where(low[v], perm(tables[0], index), perm(tables[1], index))
                    w = (u * u - 1.0) * (reach * reach) * strength
                    for q in range(3):
                        sums[q * 2 + v] = sums[q * 2 + v] + w * d[q]
            return tuple(sums)

        zero = jnp.zeros((8, 128), F32)
        return lax.fori_loop(0, 27, add, (zero,) * 6, unroll=3)

    def unlane(ref, q, value):
        for part in range(8):
            for v in range(2):
                k = (part % 4) * 4 + v * 2 + part // 4
                piece = roll(value[v], -16 * part) if part else value[v]
                ref[pl.ds(q * 128 + k, 8, stride=16), :] = piece[:, :16]

    pack(0)
    pl.semaphore_wait(barrier, len(partners))
    pending = []
    for s in range(STEPS):
        copies = send(s)
        pending += copies
        for copy in copies:
            copy.wait_recv()
        if s == 0:
            pair_weights()
        state = assemble(s)
        force = forces(state)
        for q in range(3):
            speed, place = [], []
            for v in range(2):
                speed.append(state[4 + q][v] + STEP_TIME * force[q * 2 + v])
                place.append(state[q][v] + STEP_TIME * speed[v])
            if s == STEPS - 1:
                unlane(vel_ref, q, speed)
                unlane(pos_ref, q, place)
            else:
                for v in range(2):
                    at = slice(v * 128, v * 128 + 128)
                    own[s + 1, q, :, at] = place[v]
                    own[s + 1, 4 + q, :, at] = speed[v]
        if s < STEPS - 1:
            for v in range(2):
                own[s + 1, 3, :, v * 128 : v * 128 + 128] = state[3][v]
            pack(s + 1)
    for copy in pending:
        copy.wait_send()


def body(coords, velocity, bead_type, eps_table, pair_list, migration):
    anywhere = pl.BlockSpec(memory_space=pl.ANY)
    vmem = pl.BlockSpec(memory_space=pltpu.VMEM)
    smem = pl.BlockSpec(memory_space=pltpu.SMEM)

    def buffer(*shape, dtype=F32):
        return pltpu.VMEM(shape, dtype)

    positions, velocities = pl.pallas_call(
        kernel,
        out_shape=(jax.ShapeDtypeStruct((384, 16), F32),) * 2,
        in_specs=[anywhere, anywhere, anywhere, vmem, anywhere, smem],
        out_specs=(vmem, vmem),
        scratch_shapes=[
            buffer(384, 16),
            buffer(384, 16),
            buffer(128, 16, dtype=jnp.int32),
            buffer(256, 16, dtype=jnp.int32),
            buffer(2, 9, 8, 256),
            buffer(2, 9, 8, 256),
            buffer(2, 2, 5, 8, 128),
            buffer(2, 2, 8, 128),
            buffer(2, 2, 8, 128),
            buffer(2, 2, 2, 5, 8, 128),
            buffer(2, 2, 2, 8, 128),
            buffer(2, 2, 2, 8, 128),
            buffer(2, 2, 2, 2, 8, 128),
            buffer(27, 3, 8, 256),
            buffer(27, 8, 256, dtype=jnp.int32),
            buffer(27, 8, 256),
            pltpu.SemaphoreType.DMA((4,)),
            pltpu.SemaphoreType.DMA((2, 19)),
            pltpu.SemaphoreType.DMA((2, 19)),
        ],
        compiler_params=pltpu.CompilerParams(
            collective_id=0, has_side_effects=True, vmem_limit_bytes=48 * 1024 * 1024
        ),
    )(
        coords.reshape(384, 16),
        velocity.reshape(384, 16),
        bead_type.reshape(128, 16),
        eps_table,
        pair_list.reshape(224, 16),
        migration.transpose(0, 2, 1),
    )
    return positions.reshape(coords.shape), velocities.reshape(velocity.shape)


def solution(mesh):
    placed = (
        P(None, None, "gx", "gy", "gz"),
        P(None, None, "gx", "gy", "gz"),
        P(None, "gx", "gy", "gz"),
        P(),
        P(None, "gx", "gy", "gz"),
        P(),
    )
    return jax.shard_map(
        body,
        mesh=mesh,
        in_specs=placed,
        out_specs=(P(None, None, "gx", "gy", "gz"), P(None, None, "gx", "gy", "gz")),
        check_vma=False,
    )
```

```python
import functools

import jax
import jax.numpy as jnp
from jax import lax
from jax.experimental import pallas as pl
from jax.experimental.pallas import tpu as pltpu
from jax.sharding import PartitionSpec as P

MESH = pl.DeviceIdType.MESH
F32 = jnp.float32
STEPS = 2
STEP_TIME = 0.02
SOFT = 0.3
NEAR = 1.0 / (2.25 + 0.3)
SCALE = ((2.25 + 0.3) / 2.25) ** 2
FAR = 1.0e3
half_shell = [
    (a, b, c) for a in (-1, 0, 1) for b in (-1, 0, 1) for c in (-1, 0, 1) if (a, b, c) > (0, 0, 0)
]


def column_lane(k):
    cx, cy = k // 4, k % 4
    return cy // 2, (cy % 2) * 64 + cx * 16


def roll(x, count):
    return pltpu.roll(x, count % 128, 1)


def perm(x, index):
    return jnp.take_along_axis(x, index, axis=1, mode="promise_in_bounds")


def halves(ref, *lead):
    return [ref[(*lead, slice(None), slice(v * 128, v * 128 + 128))] for v in range(2)]


def kernel(
    coords_hbm, velocity_hbm, type_hbm, eps_hbm, pairs_hbm, lists_hbm,
    pos_ref, vel_ref,
    raw_c, raw_v, raw_t, raw_p, eps_ref, lists_ref,
    own, par, sy, zo, zy, ry, rz, ryz, r2,
    near_x, near_yz, near_type, away,
    in_sem, send_sem, recv_sem,
):
    gx, gy, gz = lax.axis_index("gx"), lax.axis_index("gy"), lax.axis_index("gz")
    ring = lax.axis_size("gy")

    def device(tx, dy, tz):
        return (
            1 - gx if tx else gx,
            lax.rem(gy + (dy + ring), ring) if dy else gy,
            1 - gz if tz else gz,
        )

    partners = [
        (tx, dy, tz)
        for dy in (1, -1, 2, -2, 0)
        for tz in (0, 1)
        for tx in (0, 1)
        if (tx, dy, tz) != (0, 0, 0)
    ]
    loads = [
        pltpu.make_async_copy(coords_hbm, raw_c, in_sem.at[0]),
        pltpu.make_async_copy(velocity_hbm, raw_v, in_sem.at[1]),
        pltpu.make_async_copy(type_hbm, raw_t, in_sem.at[2]),
        pltpu.make_async_copy(pairs_hbm, raw_p.at[pl.ds(0, 224)], in_sem.at[3]),
        pltpu.make_async_copy(eps_hbm, eps_ref, in_sem.at[4]),
        pltpu.make_async_copy(lists_hbm, lists_ref, in_sem.at[5]),
    ]
    for load in loads:
        load.start()
    barrier = pltpu.get_barrier_semaphore()
    for partner in partners:
        pl.semaphore_signal(barrier, inc=1, device_id=device(*partner), device_id_type=MESH)

    raw_p[pl.ds(224, 32), :] = jnp.zeros((32, 16), jnp.int32)
    for load in loads:
        load.wait()
    lane = lax.broadcasted_iota(jnp.int32, (8, 128), 1)
    z = lane & 15
    group = lane & ~15
    cx = (lane >> 4) & 3
    lower = lane < 64
    swapped = jnp.where(z == 15, 0, 1)
    slot = (lane >> 1) & 7

    tables = []
    tiled = [jnp.concatenate([eps_ref[r : r + 1, :]] * 8, axis=1) for r in range(16)]
    tiled = [jnp.broadcast_to(row, (8, 128)) for row in tiled]
    for h in range(2):
        direct = jnp.zeros((8, 128), F32)
        transposed = jnp.zeros((8, 128), F32)
        for r in range(8):
            direct = jnp.where((lane >> 4) == r, tiled[8 * h + r], direct)
        for c in range(16):
            transposed = jnp.where(z == c, perm(tiled[c], (lane >> 4) + 8 * h), transposed)
        tables.append((0.5 * SCALE) * (direct + transposed))

    sources = [(raw_c, 0), (raw_c, 1), (raw_c, 2), (raw_t, 0), (raw_v, 0), (raw_v, 1), (raw_v, 2), (raw_p, 0), (raw_p, 1)]
    for q, (raw, block) in enumerate(sources):
        for v in range(2):
            pieces = []
            for part in range(8):
                k = (part % 4) * 4 + v * 2 + part // 4
                pieces.append(raw[pl.ds(block * 128 + k, 8, stride=16), :])
            own[0, q, :, v * 128 : v * 128 + 128] = jnp.concatenate(pieces, axis=1).astype(F32)

    def pack(s):
        state = [halves(own, s, q) for q in range(9 if s == 0 else 7)]
        ends = group + 15 * (lane & 1)
        for d in range(2):

            def pair(first, second):
                if d == 0:
                    return jnp.where(lower, roll(state[second][1], 64), state[first][1])
                return jnp.where(lower, state[first][0], roll(state[second][0], 64))

            a, b = pair(0, 1), pair(2, 3)
            listed = []
            for rows in ((0, 1, 2, 3), (4, 5, 6)):
                out = jnp.zeros((8, 128), F32)
                for m in range(2):
                    k = lists_ref[s, m, 2 + d]
                    in_second = (k & 3) >= 2
                    index = (k & 1) * 64 + (k >> 2) * 16 + z
                    for i, q in enumerate(rows):
                        value = jnp.where(in_second, state[q][1], state[q][0])
                        out = jnp.where((lane >> 4) == (2 * i + m) ^ (4 * d), perm(value, index), out)
                listed.append(out)
            sy[s, d, 1] = listed[0]
            sy[s, d, 2] = a
            sy[s, d, 3] = b
            sy[s, d, 4] = listed[1]
            thin = jnp.zeros((8, 128), F32)
            slots = [a, b, listed[0]]
            if s == 0:
                p = pair(7, 8)
                sy[s, d, 0] = p
                slots.append(p)
            for i, value in enumerate(slots):
                thin = jnp.where(slot == i + 4 * d, perm(value, ends), thin)
            zy[s, d] = thin
        for part, rows in enumerate(((0, 1, 2, 3), (7, 8))[: 2 if s == 0 else 1]):
            thin = jnp.zeros((8, 128), F32)
            for i, q in enumerate(rows):
                for v in range(2):
                    thin = jnp.where(slot == 2 * i + v, perm(state[q][v], ends), thin)
            zo[s, part] = thin

    def send(s):
        first = 0 if s == 0 else 1
        plan = []
        for d, dy in ((0, 1), (1, -1)):
            wide, narrow = pl.ds(first, 5 - first), pl.ds(first, 4 - first)
            plan.append(((0, dy, 0), sy.at[s, d, wide], ry.at[s, 0, d, wide]))
            plan.append(((1, dy, 0), sy.at[s, d, narrow], ry.at[s, 1, d, narrow]))
            for tx in range(2):
                plan.append(((tx, dy, 1), zy.at[s, d], ryz.at[s, tx, d]))
        for d, dy in ((0, 2), (1, -2)):
            for tx in range(2):
                for tz in range(2):
                    plan.append(((tx, dy, tz), zy.at[s, d] if tz else sy.at[s, d, 1], r2.at[s, tx, tz, d]))
        parts = pl.ds(0, 2 if s == 0 else 1)
        for tx in range(2):
            plan.append(((tx, 0, 1), zo.at[s, parts], rz.at[s, tx, parts]))
        rows = pl.ds(0, 9 if s == 0 else 7)
        plan.append(((1, 0, 0), own.at[s, rows], par.at[s, rows]))
        copies = []
        for i, (to, src, dst) in enumerate(plan):
            copy = pltpu.make_async_remote_copy(
                src_ref=src,
                dst_ref=dst,
                send_sem=send_sem.at[s, i],
                recv_sem=recv_sem.at[s, i],
                device_id=device(*to),
                device_id_type=MESH,
            )
            copy.start()
            copies.append(copy)
        return copies

    edge_x = {1: cx == 3, -1: cx == 0}

    def along_x(two, a):
        if a == 0:
            return two[0]
        return jnp.where(edge_x[a], roll(two[1], 48 * a), roll(two[0], -16 * a))

    def along_z(value, beyond, c):
        if c == 0:
            return value
        return jnp.where(z == (15 if c == 1 else 0), beyond, roll(value, -c))

    def four(rows):
        p0, p1, y = rows
        return [p0, p1, jnp.where(lower, y, p0), jnp.where(lower, p1, y)]

    def twisted(p0, p1):
        return [roll(jnp.where(lower, p1, p0), 64), roll(jnp.where(lower, p0, p1), 64)]

    uses = {0: (0, 1), 1: (1, 2), -1: (0, 3)}

    def pair_weights():
        row = lax.broadcasted_iota(jnp.int32, (8, 128), 0)
        power = [jnp.left_shift(1, row + 8 * g).astype(F32) for g in range(2)]

        def total(value):
            return jnp.broadcast_to(jnp.sum(value, axis=0, keepdims=True), (8, 128))

        rows, thin_rows, thin_edges = [], [], []
        for dx in range(2):
            src = own.at[0] if dx == 0 else par.at[0]
            planes = [halves(src, q) for q in (7, 8)]
            p = [total(planes[0][v] * power[0] + planes[1][v] * power[1]) for v in range(2)]
            far = [
                total(ry[0, dx, d, 0] * jnp.where(lower, power[1 - d], power[d])) for d in range(2)
            ]
            y = jnp.where(lower, far[1], far[0])
            y = y + roll(jnp.where(lower, far[0], far[1]), 64)
            rows.append([p[0], p[1], y])
            thin = total(rz[0, dx, 1] * jnp.where(slot < 2, power[0], power[1]))
            thin_rows.append(thin + roll(thin, -4))
            thin = jnp.where(slot < 4, ryz[0, dx, 0], ryz[0, dx, 1])
            thin = total(thin * jnp.where((slot < 4) == lower, power[1], power[0]))
            thin_edges.append(thin + roll(thin, 64))
        mine = [value.astype(jnp.int32) for value in rows[0][:2]]
        mine_twisted = [value.astype(jnp.int32) for value in twisted(rows[0][0], rows[0][1])]
        for a in (-1, 0, 1):
            near = [along_x([rows[0][i], rows[1][i]], a) for i in range(3)]
            other, other_edge = along_x(thin_rows, a), along_x(thin_edges, a)
            beyond = [perm(other, group + 2 * v + swapped) for v in range(2)]
            beyond.append(perm(other_edge, group + jnp.where(lower, 14, 6) + swapped))
            for c in (-1, 0, 1):
                shifted = None
                for b in (-1, 0, 1):
                    offset = (a, b, c)
                    if offset >= (0, 0, 0):
                        number = 0 if offset == (0, 0, 0) else 1 + half_shell.index(offset)
                        two = mine if b == 0 else mine_twisted
                    else:
                        number = 1 + half_shell.index((-a, -b, -c))
                        if shifted is None:
                            shifted = four([along_z(near[i], beyond[i], c).astype(jnp.int32) for i in range(3)])
                        two = [shifted[i] for i in uses[b]]
                    for v in range(2):
                        listed = ((two[v] >> number) & 1) == 1
                        away[3 * a + c + 4, b + 1, v] = jnp.where(listed, F32(a), F32(FAR))

    def assemble(s):
        listed = [[lists_ref[s, m, d] for m in range(2)] for d in range(4)]

        def member(k, names):
            out = k == names[0]
            for name in names[1:]:
                out = out | (k == name)
            return out

        def first(k, d):
            return jnp.where(k == listed[d][1], 16, 0)

        both = listed[0] + listed[1]
        column = [cx * 4 + (lane >> 6) + 2 * v for v in range(2)]
        swap = [member(k, both) for k in column]
        back = [member(k, listed[3]) for k in column]
        moved = [member(k, listed[2]) | back[v] for v, k in enumerate(column)]
        place = [first(k, 2) + first(k, 3) + z for k in column]
        index = [
            [place[v] + jnp.where(back[v], 64, 0) for v in range(2)],
            [place[v] + jnp.where(back[v], 0, 64) for v in range(2)],
        ]
        k = cx * 4 + jnp.where(lower, 0, 3)
        swap_y = member(k, both)
        hit = [member(k, listed[2]), member(k, listed[3])]
        far_y = (hit[1] & lower) | (hit[0] & ~lower)
        self_y = (hit[0] & lower) | (hit[1] & ~lower)
        place_y = jnp.where(lower, first(k, 3) + 64, first(k, 2)) + z
        index_y = [place_y, place_y ^ 64]
        end = lane & 1
        k = cx * 4 + (lane >> 6) + 2 * (slot & 1)
        swap_o = member(k, both)
        hit_o = member(k, listed[3])
        moved_o = member(k, listed[2]) | hit_o
        index_o = ((slot >> 1) * 32) + first(k, 2) + first(k, 3) + end
        index_o = jnp.where(hit_o, (index_o ^ 64) + 12, index_o + 4)
        behind = slot < 4
        half = jnp.where(behind, 1, 0) ^ (lane >> 6)
        q_r = 2 * (slot & 1) + half
        k = cx * 4 + jnp.where(behind, 3, 0)
        swap_r = member(k, both)
        hit = [member(k, listed[2]), member(k, listed[3])]
        far_r = (hit[0] & behind) | (hit[1] & ~behind)
        self_r = (hit[1] & behind) | (hit[0] & ~behind)
        index_r = jnp.where(behind, q_r * 32 + first(k, 2) + 4, ((q_r * 32) ^ 64) + first(k, 3) + 12) + end
        index_s = cx * 16 + 4 * q_r + end + jnp.where(behind, 66, 0)

        thin_rows, thin_edges = [], []
        merged = [
            jnp.where(behind, ryz[s, dx, 0], ryz[s, dx, 1]) for dx in range(2)
        ]
        ends = [rz[s, dx, 0] for dx in range(2)]
        for dx in range(2):
            value = jnp.where(moved_o, perm(merged[dx], index_o), ends[dx])
            thin_rows.append(jnp.where(swap_o, ends[1 - dx], value))
            beyond = jnp.where(behind, r2[s, dx, 1, 0], r2[s, dx, 1, 1])
            value = jnp.where(far_r, perm(beyond, index_r), merged[dx])
            value = jnp.where(self_r, perm(ends[dx], index_s), value)
            thin_edges.append(jnp.where(swap_r, merged[1 - dx], value))
        other = {a: along_x(thin_rows, a) for a in (-1, 0, 1)}
        other_edge = {a: along_x(thin_edges, a) for a in (-1, 0, 1)}

        near_list = [[ry[s, dx, d, 1] for d in range(2)] for dx in range(2)]
        far_list = [[r2[s, dx, 0, d] for d in range(2)] for dx in range(2)]

        def mix(two, q):
            return jnp.where(lower, two[q // 2], two[1 - q // 2])

        state = [None] * 7
        for q in range(4):
            plane = [halves(own, s, q), halves(par, s, q)]
            edge = []
            for dx in range(2):
                packed = [ry[s, dx, d, 2 + q // 2] for d in range(2)]
                if q % 2:
                    edge.append(roll(jnp.where(lower, packed[0], packed[1]), 64))
                else:
                    edge.append(jnp.where(lower, packed[1], packed[0]))
            odd = 32 * (q % 2)
            rows = []
            for dx in range(2):
                source = mix(near_list[dx], q)
                p = []
                for v in range(2):
                    value = jnp.where(moved[v], perm(source, index[q // 2][v] + odd), plane[dx][v])
                    p.append(jnp.where(swap[v], plane[1 - dx][v], value))
                y = jnp.where(far_y, perm(mix(far_list[dx], q), index_y[q // 2] + odd), edge[dx])
                y = jnp.where(self_y, jnp.where(lower, plane[dx][0], plane[dx][1]), y)
                rows.append([p[0], p[1], jnp.where(swap_y, edge[1 - dx], y)])
            state[q] = rows[0][:2]
            from_edge = cx * 16 + 2 * (q // 2) + swapped + jnp.where(lower, 64 * (q % 2) + 8, 64 * (1 - q % 2))
            for a in (-1, 0, 1):
                near = [along_x([rows[0][i], rows[1][i]], a) for i in range(3)]
                beyond = [perm(other[a], group + (4 * q + 2 * v) + swapped) for v in range(2)]
                beyond.append(perm(other_edge[a], from_edge))
                for c in (-1, 0, 1):
                    values = [along_z(near[i], beyond[i], c) for i in range(3)]
                    ac = 3 * a + c + 4
                    if q == 2 and c:
                        values = [value + F32(c) for value in values]
                    if q == 3:
                        values = [value.astype(jnp.int32) for value in values]
                    values = four(values)
                    if q == 0:
                        for b in (-1, 0, 1):
                            for v in range(2):
                                near_x[ac, b + 1, v] = values[uses[b][v]] + away[ac, b + 1, v]
                    else:
                        for i in range(4):
                            if q == 3:
                                near_type[ac, i] = values[i]
                            else:
                                near_yz[q - 1, ac, i] = values[i]
        speeds = [[ry[s, 0, d, 4] for d in range(2)], None]
        for q in range(3):
            mine, theirs = halves(own, s, 4 + q), halves(par, s, 4 + q)
            state[4 + q] = []
            for v in range(2):
                value = perm(mix(speeds[0], q), index[q // 2][v] + 32 * (q % 2))
                value = jnp.where(moved[v], value, mine[v])
                state[4 + q].append(jnp.where(swap[v], theirs[v], value))
        return state

    def forces(state):
        beads = [state[q] + twisted(state[q][0], state[q][1]) for q in range(4)]
        kinds = [value.astype(jnp.int32) for value in beads[3]]
        base = [(value & 7) * 16 for value in kinds]
        low = [value < 8 for value in kinds]
        beads_y = {b: [value - F32(b) if b else value for value in beads[1]] for b in (-1, 0, 1)}

        def add(ac, sums):
            sums = list(sums)
            for b in (-1, 0, 1):
                for v in range(2):
                    i = v if b == 0 else 2 + v
                    at = uses[b][v]
                    for j in range(8):
                        def bead(ref, *lead):
                            return jnp.broadcast_to(ref[(*lead, slice(j, j + 1), slice(None))], (8, 128))

                        d = [
                            beads[0][i] - bead(near_x, ac, b + 1, v),
                            beads_y[b][i] - bead(near_yz, 0, ac, at),
                            beads[2][i] - bead(near_yz, 1, ac, at),
                        ]
                        apart = d[0] * d[0] + d[1] * d[1] + (d[2] * d[2] + SOFT)
                        u = pl.reciprocal(apart, approx=True)
                        reach = jnp.maximum(u - NEAR, 0.0)
                        index = base[i] + bead(near_type, ac, at)
                        strength = jnp.where(low[i], perm(tables[0], index), perm(tables[1], index))
                        w = (u * u - 1.0) * (reach * reach) * strength
                        for q in range(3):
                            sums[q * 4 + i] = sums[q * 4 + i] + w * d[q]
            return tuple(sums)

        zero = jnp.zeros((8, 128), F32)
        sums = lax.fori_loop(0, 9, add, (zero,) * 12, unroll=9)
        force = []
        for q in range(3):
            p0, p1, t1, t2 = sums[4 * q : 4 * q + 4]
            force.append([
                p0 + roll(jnp.where(lower, t1, t2), 64),
                p1 + roll(jnp.where(lower, t2, t1), 64),
            ])
        return force

    pack(0)
    pl.semaphore_wait(barrier, len(partners))
    pending = []
    for s in range(STEPS):
        copies = send(s)
        pending += copies
        for copy in copies:
            copy.wait_recv()
        if s == 0:
            pair_weights()
        state = assemble(s)
        force = forces(state)
        for q in range(3):
            speed, place = [], []
            for v in range(2):
                speed.append(state[4 + q][v] + STEP_TIME * force[q][v])
                place.append(state[q][v] + STEP_TIME * speed[v])
            if s == STEPS - 1:
                for v in range(2):
                    at = slice(v * 128, v * 128 + 128)
                    vel_ref[q, :, at] = speed[v]
                    pos_ref[q, :, at] = place[v]
            else:
                for v in range(2):
                    at = slice(v * 128, v * 128 + 128)
                    own[s + 1, q, :, at] = place[v]
                    own[s + 1, 4 + q, :, at] = speed[v]
        if s < STEPS - 1:
            for v in range(2):
                own[s + 1, 3, :, v * 128 : v * 128 + 128] = state[3][v]
            pack(s + 1)
    for copy in pending:
        copy.wait_send()


def finish(*refs):
    for value_ref, ref in zip(refs[:2], refs[2:]):
        for q in range(3):
            value = halves(value_ref, q)
            for part in range(8):
                for v in range(2):
                    k = (part % 4) * 4 + v * 2 + part // 4
                    piece = roll(value[v], -16 * part) if part else value[v]
                    ref[pl.ds(q * 128 + k, 8, stride=16), :] = piece[:, :16]


def body(coords, velocity, bead_type, eps_table, pair_list, migration):
    hbm = pl.BlockSpec(memory_space=pltpu.HBM)
    vmem = pl.BlockSpec(memory_space=pltpu.VMEM)

    def buffer(*shape, dtype=F32):
        return pltpu.VMEM(shape, dtype)

    positions, velocities = pl.pallas_call(
        kernel,
        out_shape=(jax.ShapeDtypeStruct((3, 8, 256), F32),) * 2,
        in_specs=[hbm] * 6,
        out_specs=(vmem, vmem),
        scratch_shapes=[
            buffer(384, 16),
            buffer(384, 16),
            buffer(128, 16, dtype=jnp.int32),
            buffer(256, 16, dtype=jnp.int32),
            buffer(16, 16),
            pltpu.SMEM((2, 2, 4), jnp.int32),
            buffer(2, 9, 8, 256),
            buffer(2, 9, 8, 256),
            buffer(2, 2, 5, 8, 128),
            buffer(2, 2, 8, 128),
            buffer(2, 2, 8, 128),
            buffer(2, 2, 2, 5, 8, 128),
            buffer(2, 2, 2, 8, 128),
            buffer(2, 2, 2, 8, 128),
            buffer(2, 2, 2, 2, 8, 128),
            buffer(9, 3, 2, 8, 128),
            buffer(2, 9, 4, 8, 128),
            buffer(9, 4, 8, 128, dtype=jnp.int32),
            buffer(9, 3, 2, 8, 128),
            pltpu.SemaphoreType.DMA((6,)),
            pltpu.SemaphoreType.DMA((2, 19)),
            pltpu.SemaphoreType.DMA((2, 19)),
        ],
        compiler_params=pltpu.CompilerParams(
            collective_id=0, has_side_effects=True
        ),
    )(
        coords.reshape(384, 16),
        velocity.reshape(384, 16),
        bead_type.reshape(128, 16),
        eps_table,
        pair_list.reshape(224, 16),
        migration.transpose(0, 2, 1),
    )
    positions, velocities = pl.pallas_call(
        finish,
        out_shape=(jax.ShapeDtypeStruct((384, 16), F32),) * 2,
        in_specs=(vmem, vmem),
        out_specs=(vmem, vmem),
    )(positions, velocities)
    return positions.reshape(coords.shape), velocities.reshape(velocity.shape)


def solution(mesh):
    placed = (
        P(None, None, "gx", "gy", "gz"),
        P(None, None, "gx", "gy", "gz"),
        P(None, "gx", "gy", "gz"),
        P(),
        P(None, "gx", "gy", "gz"),
        P(),
    )
    return jax.shard_map(
        body,
        mesh=mesh,
        in_specs=placed,
        out_specs=(P(None, None, "gx", "gy", "gz"), P(None, None, "gx", "gy", "gz")),
        check_vma=False,
    )
```

```python
import functools

import jax
import jax.numpy as jnp
from jax import lax
from jax.experimental import pallas as pl
from jax.experimental.pallas import tpu as pltpu
from jax.sharding import PartitionSpec as P

MESH = pl.DeviceIdType.MESH
F32 = jnp.float32
STEPS = 2
STEP_TIME = 0.02
SOFT = 0.3
NEAR = 1.0 / (2.25 + 0.3)
UNIT = ((2.25 + 0.3) / 2.25) ** 2 * 2.0 / 65535.0
FAR = 1.0e3
half_shell = [
    (a, b, c) for a in (-1, 0, 1) for b in (-1, 0, 1) for c in (-1, 0, 1) if (a, b, c) > (0, 0, 0)
]


def column_lane(k):
    cx, cy = k // 4, k % 4
    return cy // 2, (cy % 2) * 64 + cx * 16


def roll(x, count):
    return pltpu.roll(x, count % 128, 1)


def perm(x, index):
    return jnp.take_along_axis(x, index, axis=1, mode="promise_in_bounds")


def halves(ref, *lead):
    return [ref[(*lead, slice(None), slice(v * 128, v * 128 + 128))] for v in range(2)]


def kernel(
    coords_hbm, velocity_hbm, type_hbm, eps_hbm, pairs_hbm, lists_hbm,
    result_hbm,
    raw_c, raw_v, raw_t, raw_p, eps_ref, lists_ref,
    own, par, sy, zo, zy, ry, rz, ryz, r2,
    near_x, near_yz, near_type, away, result, out_sem,
    in_sem, send_sem, recv_sem,
):
    gx, gy, gz = lax.axis_index("gx"), lax.axis_index("gy"), lax.axis_index("gz")
    ring = lax.axis_size("gy")

    def device(tx, dy, tz):
        return (
            1 - gx if tx else gx,
            lax.rem(gy + (dy + ring), ring) if dy else gy,
            1 - gz if tz else gz,
        )

    partners = [
        (tx, dy, tz)
        for dy in (1, -1, 2, -2, 0)
        for tz in (0, 1)
        for tx in (0, 1)
        if (tx, dy, tz) != (0, 0, 0)
    ]
    loads = [
        pltpu.make_async_copy(coords_hbm, raw_c, in_sem.at[0]),
        pltpu.make_async_copy(velocity_hbm, raw_v, in_sem.at[1]),
        pltpu.make_async_copy(type_hbm, raw_t, in_sem.at[2]),
        pltpu.make_async_copy(pairs_hbm, raw_p.at[pl.ds(0, 224)], in_sem.at[3]),
        pltpu.make_async_copy(eps_hbm, eps_ref, in_sem.at[4]),
        pltpu.make_async_copy(lists_hbm, lists_ref, in_sem.at[5]),
    ]
    for load in loads:
        load.start()
    barrier = pltpu.get_barrier_semaphore()
    for partner in partners:
        pl.semaphore_signal(barrier, inc=1, device_id=device(*partner), device_id_type=MESH)

    raw_p[pl.ds(224, 32), :] = jnp.zeros((32, 16), jnp.int32)
    for load in loads:
        load.wait()
    lane = lax.broadcasted_iota(jnp.int32, (8, 128), 1)
    z = lane & 15
    group = lane & ~15
    cx = (lane >> 4) & 3
    lower = lane < 64
    swapped = jnp.where(z == 15, 0, 1)
    slot = (lane >> 1) & 7

    tables = []
    tiled = [jnp.concatenate([eps_ref[r : r + 1, :]] * 8, axis=1) for r in range(16)]
    tiled = [jnp.broadcast_to(row, (8, 128)) for row in tiled]
    for h in range(2):
        direct = jnp.zeros((8, 128), F32)
        transposed = jnp.zeros((8, 128), F32)
        for r in range(8):
            direct = jnp.where((lane >> 4) == r, tiled[8 * h + r], direct)
        for c in range(16):
            transposed = jnp.where(z == c, perm(tiled[c], (lane >> 4) + 8 * h), transposed)
        tables.append((direct + transposed) * (65535.0 / 4.0) + 0.5)

    high, rest = [value.astype(jnp.int32) for value in tables]
    table = (high << 16) | rest

    sources = [(raw_c, 0), (raw_c, 1), (raw_c, 2), (raw_t, 0), (raw_v, 0), (raw_v, 1), (raw_v, 2), (raw_p, 0), (raw_p, 1)]
    for q, (raw, block) in enumerate(sources):
        for v in range(2):
            pieces = []
            for part in range(8):
                k = (part % 4) * 4 + v * 2 + part // 4
                pieces.append(raw[pl.ds(block * 128 + k, 8, stride=16), :])
            own[0, q, :, v * 128 : v * 128 + 128] = jnp.concatenate(pieces, axis=1).astype(F32)

    def pack(s):
        state = [halves(own, s, q) for q in range(9 if s == 0 else 7)]
        ends = group + 15 * (lane & 1)
        for d in range(2):

            def pair(first, second):
                if d == 0:
                    return jnp.where(lower, roll(state[second][1], 64), state[first][1])
                return jnp.where(lower, state[first][0], roll(state[second][0], 64))

            a, b = pair(0, 1), pair(2, 3)
            listed = []
            for rows in ((0, 1, 2, 3), (4, 5, 6)):
                out = jnp.zeros((8, 128), F32)
                for m in range(2):
                    k = lists_ref[s, m, 2 + d]
                    in_second = (k & 3) >= 2
                    index = (k & 1) * 64 + (k >> 2) * 16 + z
                    for i, q in enumerate(rows):
                        value = jnp.where(in_second, state[q][1], state[q][0])
                        out = jnp.where((lane >> 4) == (2 * i + m) ^ (4 * d), perm(value, index), out)
                listed.append(out)
            sy[s, d, 1] = listed[0]
            sy[s, d, 2] = a
            sy[s, d, 3] = b
            sy[s, d, 4] = listed[1]
            thin = jnp.zeros((8, 128), F32)
            slots = [a, b, listed[0]]
            if s == 0:
                p = pair(7, 8)
                sy[s, d, 0] = p
                slots.append(p)
            for i, value in enumerate(slots):
                thin = jnp.where(slot == i + 4 * d, perm(value, ends), thin)
            zy[s, d] = thin
        for part, rows in enumerate(((0, 1, 2, 3), (7, 8))[: 2 if s == 0 else 1]):
            thin = jnp.zeros((8, 128), F32)
            for i, q in enumerate(rows):
                for v in range(2):
                    thin = jnp.where(slot == 2 * i + v, perm(state[q][v], ends), thin)
            zo[s, part] = thin

    def send(s):
        first = 0 if s == 0 else 1
        plan = []
        for d, dy in ((0, 1), (1, -1)):
            wide, narrow = pl.ds(first, 5 - first), pl.ds(first, 4 - first)
            plan.append(((0, dy, 0), sy.at[s, d, wide], ry.at[s, 0, d, wide]))
            plan.append(((1, dy, 0), sy.at[s, d, narrow], ry.at[s, 1, d, narrow]))
            for tx in range(2):
                plan.append(((tx, dy, 1), zy.at[s, d], ryz.at[s, tx, d]))
        for d, dy in ((0, 2), (1, -2)):
            for tx in range(2):
                for tz in range(2):
                    plan.append(((tx, dy, tz), zy.at[s, d] if tz else sy.at[s, d, 1], r2.at[s, tx, tz, d]))
        parts = pl.ds(0, 2 if s == 0 else 1)
        for tx in range(2):
            plan.append(((tx, 0, 1), zo.at[s, parts], rz.at[s, tx, parts]))
        rows = pl.ds(0, 9 if s == 0 else 7)
        plan.append(((1, 0, 0), own.at[s, rows], par.at[s, rows]))
        copies = []
        for i, (to, src, dst) in enumerate(plan):
            copy = pltpu.make_async_remote_copy(
                src_ref=src,
                dst_ref=dst,
                send_sem=send_sem.at[s, i],
                recv_sem=recv_sem.at[s, i],
                device_id=device(*to),
                device_id_type=MESH,
            )
            copy.start()
            copies.append(copy)
        return copies

    edge_x = {1: cx == 3, -1: cx == 0}

    def along_x(two, a):
        if a == 0:
            return two[0]
        return jnp.where(edge_x[a], roll(two[1], 48 * a), roll(two[0], -16 * a))

    def along_z(value, beyond, c):
        if c == 0:
            return value
        return jnp.where(z == (15 if c == 1 else 0), beyond, roll(value, -c))

    def four(rows):
        p0, p1, y = rows
        return [p0, p1, jnp.where(lower, y, p0), jnp.where(lower, p1, y)]

    def twisted(p0, p1):
        return [roll(jnp.where(lower, p1, p0), 64), roll(jnp.where(lower, p0, p1), 64)]

    uses = {0: (0, 1), 1: (1, 2), -1: (0, 3)}

    def pair_weights():
        row = lax.broadcasted_iota(jnp.int32, (8, 128), 0)
        power = [jnp.left_shift(1, row + 8 * g).astype(F32) for g in range(2)]

        def total(value):
            return jnp.broadcast_to(jnp.sum(value, axis=0, keepdims=True), (8, 128))

        rows, thin_rows, thin_edges = [], [], []
        for dx in range(2):
            src = own.at[0] if dx == 0 else par.at[0]
            planes = [halves(src, q) for q in (7, 8)]
            p = [total(planes[0][v] * power[0] + planes[1][v] * power[1]) for v in range(2)]
            far = [
                total(ry[0, dx, d, 0] * jnp.where(lower, power[1 - d], power[d])) for d in range(2)
            ]
            y = jnp.where(lower, far[1], far[0])
            y = y + roll(jnp.where(lower, far[0], far[1]), 64)
            rows.append([p[0], p[1], y])
            thin = total(rz[0, dx, 1] * jnp.where(slot < 2, power[0], power[1]))
            thin_rows.append(thin + roll(thin, -4))
            thin = jnp.where(slot < 4, ryz[0, dx, 0], ryz[0, dx, 1])
            thin = total(thin * jnp.where((slot < 4) == lower, power[1], power[0]))
            thin_edges.append(thin + roll(thin, 64))
        mine = [value.astype(jnp.int32) for value in rows[0][:2]]
        mine_twisted = [value.astype(jnp.int32) for value in twisted(rows[0][0], rows[0][1])]
        for a in (-1, 0, 1):
            near = [along_x([rows[0][i], rows[1][i]], a) for i in range(3)]
            other, other_edge = along_x(thin_rows, a), along_x(thin_edges, a)
            beyond = [perm(other, group + 2 * v + swapped) for v in range(2)]
            beyond.append(perm(other_edge, group + jnp.where(lower, 14, 6) + swapped))
            for c in (-1, 0, 1):
                shifted = None
                for b in (-1, 0, 1):
                    offset = (a, b, c)
                    if offset >= (0, 0, 0):
                        number = 0 if offset == (0, 0, 0) else 1 + half_shell.index(offset)
                        two = mine if b == 0 else mine_twisted
                    else:
                        number = 1 + half_shell.index((-a, -b, -c))
                        if shifted is None:
                            shifted = four([along_z(near[i], beyond[i], c).astype(jnp.int32) for i in range(3)])
                        two = [shifted[i] for i in uses[b]]
                    for v in range(2):
                        listed = ((two[v] >> number) & 1) == 1
                        away[3 * a + c + 4, b + 1, v] = jnp.where(listed, F32(a), F32(FAR))

    def assemble(s):
        listed = [[lists_ref[s, m, d] for m in range(2)] for d in range(4)]

        def member(k, names):
            out = k == names[0]
            for name in names[1:]:
                out = out | (k == name)
            return out

        def first(k, d):
            return jnp.where(k == listed[d][1], 16, 0)

        both = listed[0] + listed[1]
        column = [cx * 4 + (lane >> 6) + 2 * v for v in range(2)]
        swap = [member(k, both) for k in column]
        back = [member(k, listed[3]) for k in column]
        moved = [member(k, listed[2]) | back[v] for v, k in enumerate(column)]
        place = [first(k, 2) + first(k, 3) + z for k in column]
        index = [
            [place[v] + jnp.where(back[v], 64, 0) for v in range(2)],
            [place[v] + jnp.where(back[v], 0, 64) for v in range(2)],
        ]
        k = cx * 4 + jnp.where(lower, 0, 3)
        swap_y = member(k, both)
        hit = [member(k, listed[2]), member(k, listed[3])]
        far_y = (hit[1] & lower) | (hit[0] & ~lower)
        self_y = (hit[0] & lower) | (hit[1] & ~lower)
        place_y = jnp.where(lower, first(k, 3) + 64, first(k, 2)) + z
        index_y = [place_y, place_y ^ 64]
        end = lane & 1
        k = cx * 4 + (lane >> 6) + 2 * (slot & 1)
        swap_o = member(k, both)
        hit_o = member(k, listed[3])
        moved_o = member(k, listed[2]) | hit_o
        index_o = ((slot >> 1) * 32) + first(k, 2) + first(k, 3) + end
        index_o = jnp.where(hit_o, (index_o ^ 64) + 12, index_o + 4)
        behind = slot < 4
        half = jnp.where(behind, 1, 0) ^ (lane >> 6)
        q_r = 2 * (slot & 1) + half
        k = cx * 4 + jnp.where(behind, 3, 0)
        swap_r = member(k, both)
        hit = [member(k, listed[2]), member(k, listed[3])]
        far_r = (hit[0] & behind) | (hit[1] & ~behind)
        self_r = (hit[1] & behind) | (hit[0] & ~behind)
        index_r = jnp.where(behind, q_r * 32 + first(k, 2) + 4, ((q_r * 32) ^ 64) + first(k, 3) + 12) + end
        index_s = cx * 16 + 4 * q_r + end + jnp.where(behind, 66, 0)

        thin_rows, thin_edges = [], []
        merged = [
            jnp.where(behind, ryz[s, dx, 0], ryz[s, dx, 1]) for dx in range(2)
        ]
        ends = [rz[s, dx, 0] for dx in range(2)]
        for dx in range(2):
            value = jnp.where(moved_o, perm(merged[dx], index_o), ends[dx])
            thin_rows.append(jnp.where(swap_o, ends[1 - dx], value))
            beyond = jnp.where(behind, r2[s, dx, 1, 0], r2[s, dx, 1, 1])
            value = jnp.where(far_r, perm(beyond, index_r), merged[dx])
            value = jnp.where(self_r, perm(ends[dx], index_s), value)
            thin_edges.append(jnp.where(swap_r, merged[1 - dx], value))
        other = {a: along_x(thin_rows, a) for a in (-1, 0, 1)}
        other_edge = {a: along_x(thin_edges, a) for a in (-1, 0, 1)}

        near_list = [[ry[s, dx, d, 1] for d in range(2)] for dx in range(2)]
        far_list = [[r2[s, dx, 0, d] for d in range(2)] for dx in range(2)]

        def mix(two, q):
            return jnp.where(lower, two[q // 2], two[1 - q // 2])

        state = [None] * 7
        for q in range(4):
            plane = [halves(own, s, q), halves(par, s, q)]
            edge = []
            for dx in range(2):
                packed = [ry[s, dx, d, 2 + q // 2] for d in range(2)]
                if q % 2:
                    edge.append(roll(jnp.where(lower, packed[0], packed[1]), 64))
                else:
                    edge.append(jnp.where(lower, packed[1], packed[0]))
            odd = 32 * (q % 2)
            rows = []
            for dx in range(2):
                source = mix(near_list[dx], q)
                p = []
                for v in range(2):
                    value = jnp.where(moved[v], perm(source, index[q // 2][v] + odd), plane[dx][v])
                    p.append(jnp.where(swap[v], plane[1 - dx][v], value))
                y = jnp.where(far_y, perm(mix(far_list[dx], q), index_y[q // 2] + odd), edge[dx])
                y = jnp.where(self_y, jnp.where(lower, plane[dx][0], plane[dx][1]), y)
                rows.append([p[0], p[1], jnp.where(swap_y, edge[1 - dx], y)])
            state[q] = rows[0][:2]
            from_edge = cx * 16 + 2 * (q // 2) + swapped + jnp.where(lower, 64 * (q % 2) + 8, 64 * (1 - q % 2))
            for a in (-1, 0, 1):
                near = [along_x([rows[0][i], rows[1][i]], a) for i in range(3)]
                beyond = [perm(other[a], group + (4 * q + 2 * v) + swapped) for v in range(2)]
                beyond.append(perm(other_edge[a], from_edge))
                for c in (-1, 0, 1):
                    values = [along_z(near[i], beyond[i], c) for i in range(3)]
                    ac = 3 * a + c + 4
                    if q == 2 and c:
                        values = [value + F32(c) for value in values]
                    if q == 3:
                        values = [value.astype(jnp.int32) for value in values]
                    values = four(values)
                    if q == 0:
                        for b in (-1, 0, 1):
                            for v in range(2):
                                near_x[ac, b + 1, v] = values[uses[b][v]] + away[ac, b + 1, v]
                    else:
                        for i in range(4):
                            if q == 3:
                                near_type[ac, i] = values[i]
                            else:
                                near_yz[q - 1, ac, i] = values[i]
        speeds = [[ry[s, 0, d, 4] for d in range(2)], None]
        for q in range(3):
            mine, theirs = halves(own, s, 4 + q), halves(par, s, 4 + q)
            state[4 + q] = []
            for v in range(2):
                value = perm(mix(speeds[0], q), index[q // 2][v] + 32 * (q % 2))
                value = jnp.where(moved[v], value, mine[v])
                state[4 + q].append(jnp.where(swap[v], theirs[v], value))
        return state

    def forces(state):
        beads = [state[q] + twisted(state[q][0], state[q][1]) for q in range(4)]
        kinds = [value.astype(jnp.int32) for value in beads[3]]
        base = [(value & 7) * 16 for value in kinds]
        lift = [(value >> 3) << 4 for value in kinds]
        beads_y = {b: [value - F32(b) if b else value for value in beads[1]] for b in (-1, 0, 1)}

        def add(ac, sums):
            sums = list(sums)
            for b in (-1, 0, 1):
                for v in range(2):
                    i = v if b == 0 else 2 + v
                    at = uses[b][v]
                    for j in range(8):
                        def bead(ref, *lead):
                            return jnp.broadcast_to(ref[(*lead, slice(j, j + 1), slice(None))], (8, 128))

                        d = [
                            beads[0][i] - bead(near_x, ac, b + 1, v),
                            beads_y[b][i] - bead(near_yz, 0, ac, at),
                            beads[2][i] - bead(near_yz, 1, ac, at),
                        ]
                        apart = d[0] * d[0] + d[1] * d[1] + (d[2] * d[2] + SOFT)
                        u = pl.reciprocal(apart, approx=True)
                        reach = jnp.maximum(u - NEAR, 0.0)
                        index = base[i] + bead(near_type, ac, at)
                        strength = lax.shift_right_logical(perm(table, index) << lift[i], 16).astype(F32)
                        w = (u * u - 1.0) * (reach * reach) * strength
                        for q in range(3):
                            sums[q * 4 + i] = sums[q * 4 + i] + w * d[q]
            return tuple(sums)

        zero = jnp.zeros((8, 128), F32)
        sums = lax.fori_loop(0, 9, add, (zero,) * 12, unroll=9)
        force = []
        for q in range(3):
            p0, p1, t1, t2 = sums[4 * q : 4 * q + 4]
            force.append([
                (p0 + roll(jnp.where(lower, t1, t2), 64)) * UNIT,
                (p1 + roll(jnp.where(lower, t2, t1), 64)) * UNIT,
            ])
        return force

    pack(0)
    pl.semaphore_wait(barrier, len(partners))
    pending = []
    for s in range(STEPS):
        copies = send(s)
        pending += copies
        for copy in copies:
            copy.wait_recv()
        if s == 0:
            pair_weights()
        state = assemble(s)
        force = forces(state)
        for q in range(3):
            speed, place = [], []
            for v in range(2):
                speed.append(state[4 + q][v] + STEP_TIME * force[q][v])
                place.append(state[q][v] + STEP_TIME * speed[v])
            if s == STEPS - 1:
                for v in range(2):
                    at = slice(v * 128, v * 128 + 128)
                    result[q, :, at] = place[v]
                    result[3 + q, :, at] = speed[v]
            else:
                for v in range(2):
                    at = slice(v * 128, v * 128 + 128)
                    own[s + 1, q, :, at] = place[v]
                    own[s + 1, 4 + q, :, at] = speed[v]
        if s < STEPS - 1:
            for v in range(2):
                own[s + 1, 3, :, v * 128 : v * 128 + 128] = state[3][v]
            pack(s + 1)
    out = pltpu.make_async_copy(result, result_hbm, out_sem)
    out.start()
    for copy in pending:
        copy.wait_send()
    out.wait()


def finish(result_hbm, pos_hbm, vel_hbm, result, pos, vel, sem):
    load = pltpu.make_async_copy(result_hbm, result, sem.at[0])
    load.start()
    load.wait()
    stores = []
    for i, (rows, out) in enumerate(((pos, pos_hbm), (vel, vel_hbm))):
        for q in range(3):
            value = halves(result, 3 * i + q)
            for part in range(8):
                for v in range(2):
                    k = (part % 4) * 4 + v * 2 + part // 4
                    piece = roll(value[v], -16 * part) if part else value[v]
                    rows[pl.ds(q * 128 + k, 8, stride=16), :] = piece[:, :16]
        stores.append(pltpu.make_async_copy(rows, out, sem.at[1 + i]))
        stores[i].start()
    for store in stores:
        store.wait()


def body(coords, velocity, bead_type, eps_table, pair_list, migration):
    hbm = pl.BlockSpec(memory_space=pltpu.HBM)

    def buffer(*shape, dtype=F32):
        return pltpu.VMEM(shape, dtype)

    result = pl.pallas_call(
        kernel,
        out_shape=jax.ShapeDtypeStruct((6, 8, 256), F32),
        in_specs=[hbm] * 6,
        out_specs=hbm,
        scratch_shapes=[
            buffer(384, 16),
            buffer(384, 16),
            buffer(128, 16, dtype=jnp.int32),
            buffer(256, 16, dtype=jnp.int32),
            buffer(16, 16),
            pltpu.SMEM((2, 2, 4), jnp.int32),
            buffer(2, 9, 8, 256),
            buffer(2, 9, 8, 256),
            buffer(2, 2, 5, 8, 128),
            buffer(2, 2, 8, 128),
            buffer(2, 2, 8, 128),
            buffer(2, 2, 2, 5, 8, 128),
            buffer(2, 2, 2, 8, 128),
            buffer(2, 2, 2, 8, 128),
            buffer(2, 2, 2, 2, 8, 128),
            buffer(9, 3, 2, 8, 128),
            buffer(2, 9, 4, 8, 128),
            buffer(9, 4, 8, 128, dtype=jnp.int32),
            buffer(9, 3, 2, 8, 128),
            buffer(6, 8, 256),
            pltpu.SemaphoreType.DMA,
            pltpu.SemaphoreType.DMA((6,)),
            pltpu.SemaphoreType.DMA((2, 19)),
            pltpu.SemaphoreType.DMA((2, 19)),
        ],
        compiler_params=pltpu.CompilerParams(
            collective_id=0, has_side_effects=True
        ),
    )(
        coords.reshape(384, 16),
        velocity.reshape(384, 16),
        bead_type.reshape(128, 16),
        eps_table,
        pair_list.reshape(224, 16),
        migration.transpose(0, 2, 1),
    )
    positions, velocities = pl.pallas_call(
        finish,
        out_shape=(jax.ShapeDtypeStruct((384, 16), F32),) * 2,
        in_specs=[hbm],
        out_specs=(hbm, hbm),
        scratch_shapes=[
            buffer(6, 8, 256),
            buffer(384, 16),
            buffer(384, 16),
            pltpu.SemaphoreType.DMA((3,)),
        ],
    )(result)
    return positions.reshape(coords.shape), velocities.reshape(velocity.shape)


def solution(mesh):
    placed = (
        P(None, None, "gx", "gy", "gz"),
        P(None, None, "gx", "gy", "gz"),
        P(None, "gx", "gy", "gz"),
        P(),
        P(None, "gx", "gy", "gz"),
        P(),
    )
    return jax.shard_map(
        body,
        mesh=mesh,
        in_specs=placed,
        out_specs=(P(None, None, "gx", "gy", "gz"), P(None, None, "gx", "gy", "gz")),
        check_vma=False,
    )
```

```python
import functools

import jax
import jax.numpy as jnp
from jax import lax
from jax.experimental import pallas as pl
from jax.experimental.pallas import tpu as pltpu
from jax.sharding import PartitionSpec as P

MESH = pl.DeviceIdType.MESH
F32 = jnp.float32
STEPS = 2
STEP_TIME = 0.02
SOFT = 0.3
NEAR = 1.0 / (2.25 + 0.3)
UNIT = ((2.25 + 0.3) / 2.25) ** 2 * 2.0 / 65535.0
FAR = 1.0e3
half_shell = [
    (a, b, c) for a in (-1, 0, 1) for b in (-1, 0, 1) for c in (-1, 0, 1) if (a, b, c) > (0, 0, 0)
]


def column_lane(k):
    cx, cy = k // 4, k % 4
    return cy // 2, (cy % 2) * 64 + cx * 16


def roll(x, count):
    return pltpu.roll(x, count % 128, 1)


def perm(x, index):
    return jnp.take_along_axis(x, index, axis=1, mode="promise_in_bounds")


def halves(ref, *lead):
    return [ref[(*lead, slice(None), slice(v * 128, v * 128 + 128))] for v in range(2)]


def kernel(
    coords_hbm, velocity_hbm, type_hbm, eps_hbm, pairs_hbm, lists_hbm,
    result_hbm,
    raw_c, raw_v, raw_t, raw_p, eps_ref, lists_ref,
    own, par, sy, zo, zy, ry, rz, ryz, r2,
    near_x, near_yz, near_type, away, result, out_sem,
    in_sem, send_sem, recv_sem,
):
    gx, gy, gz = lax.axis_index("gx"), lax.axis_index("gy"), lax.axis_index("gz")
    ring = lax.axis_size("gy")

    def device(tx, dy, tz):
        return (
            1 - gx if tx else gx,
            lax.rem(gy + (dy + ring), ring) if dy else gy,
            1 - gz if tz else gz,
        )

    partners = [
        (tx, dy, tz)
        for dy in (1, -1, 2, -2, 0)
        for tz in (0, 1)
        for tx in (0, 1)
        if (tx, dy, tz) != (0, 0, 0)
    ]
    loads = [
        pltpu.make_async_copy(coords_hbm, raw_c, in_sem.at[0]),
        pltpu.make_async_copy(velocity_hbm, raw_v, in_sem.at[1]),
        pltpu.make_async_copy(type_hbm, raw_t, in_sem.at[2]),
        pltpu.make_async_copy(pairs_hbm, raw_p.at[pl.ds(0, 224)], in_sem.at[3]),
        pltpu.make_async_copy(eps_hbm, eps_ref, in_sem.at[4]),
        pltpu.make_async_copy(lists_hbm, lists_ref, in_sem.at[5]),
    ]
    for load in loads:
        load.start()
    barrier = pltpu.get_barrier_semaphore()
    for partner in partners:
        pl.semaphore_signal(barrier, inc=1, device_id=device(*partner), device_id_type=MESH)

    raw_p[pl.ds(224, 32), :] = jnp.zeros((32, 16), jnp.int32)
    for load in loads:
        load.wait()
    lane = lax.broadcasted_iota(jnp.int32, (8, 128), 1)
    z = lane & 15
    group = lane & ~15
    cx = (lane >> 4) & 3
    lower = lane < 64
    swapped = jnp.where(z == 15, 0, 1)
    slot = (lane >> 1) & 7

    def strengths():
        tables = []
        tiled = [jnp.concatenate([eps_ref[r : r + 1, :]] * 8, axis=1) for r in range(16)]
        tiled = [jnp.broadcast_to(row, (8, 128)) for row in tiled]
        for h in range(2):
            direct = jnp.zeros((8, 128), F32)
            transposed = jnp.zeros((8, 128), F32)
            for r in range(8):
                direct = jnp.where((lane >> 4) == r, tiled[8 * h + r], direct)
            for c in range(16):
                transposed = jnp.where(z == c, perm(tiled[c], (lane >> 4) + 8 * h), transposed)
            tables.append((direct + transposed) * (65535.0 / 4.0) + 0.5)

        high, rest = [value.astype(jnp.int32) for value in tables]
        table = (high << 16) | rest
        return table

    sources = [(raw_c, 0), (raw_c, 1), (raw_c, 2), (raw_t, 0), (raw_v, 0), (raw_v, 1), (raw_v, 2), (raw_p, 0), (raw_p, 1)]
    for q, (raw, block) in enumerate(sources):
        for v in range(2):
            pieces = []
            for part in range(8):
                k = (part % 4) * 4 + v * 2 + part // 4
                pieces.append(raw[pl.ds(block * 128 + k, 8, stride=16), :])
            own[0, q, :, v * 128 : v * 128 + 128] = jnp.concatenate(pieces, axis=1).astype(F32)

    def pack(s):
        state = [halves(own, s, q) for q in range(9 if s == 0 else 7)]
        ends = group + 15 * (lane & 1)
        for d in range(2):

            def pair(first, second):
                if d == 0:
                    return jnp.where(lower, roll(state[second][1], 64), state[first][1])
                return jnp.where(lower, state[first][0], roll(state[second][0], 64))

            a, b = pair(0, 1), pair(2, 3)
            listed = []
            for rows in ((0, 1, 2, 3), (4, 5, 6)):
                out = jnp.zeros((8, 128), F32)
                for m in range(2):
                    k = lists_ref[s, m, 2 + d]
                    in_second = (k & 3) >= 2
                    index = (k & 1) * 64 + (k >> 2) * 16 + z
                    for i, q in enumerate(rows):
                        value = jnp.where(in_second, state[q][1], state[q][0])
                        out = jnp.where((lane >> 4) == (2 * i + m) ^ (4 * d), perm(value, index), out)
                listed.append(out)
            sy[s, d, 1] = listed[0]
            sy[s, d, 2] = a
            sy[s, d, 3] = b
            sy[s, d, 4] = listed[1]
            thin = jnp.zeros((8, 128), F32)
            slots = [a, b, listed[0]]
            if s == 0:
                p = pair(7, 8)
                sy[s, d, 0] = p
                slots.append(p)
            for i, value in enumerate(slots):
                thin = jnp.where(slot == i + 4 * d, perm(value, ends), thin)
            zy[s, d] = thin
        for part, rows in enumerate(((0, 1, 2, 3), (7, 8))[: 2 if s == 0 else 1]):
            thin = jnp.zeros((8, 128), F32)
            for i, q in enumerate(rows):
                for v in range(2):
                    thin = jnp.where(slot == 2 * i + v, perm(state[q][v], ends), thin)
            zo[s, part] = thin

    def send(s):
        first = 0 if s == 0 else 1
        plan = []
        for d, dy in ((0, 1), (1, -1)):
            wide, narrow = pl.ds(first, 5 - first), pl.ds(first, 4 - first)
            plan.append(((0, dy, 0), sy.at[s, d, wide], ry.at[s, 0, d, wide]))
            plan.append(((1, dy, 0), sy.at[s, d, narrow], ry.at[s, 1, d, narrow]))
            for tx in range(2):
                plan.append(((tx, dy, 1), zy.at[s, d], ryz.at[s, tx, d]))
        for d, dy in ((0, 2), (1, -2)):
            for tx in range(2):
                for tz in range(2):
                    plan.append(((tx, dy, tz), zy.at[s, d] if tz else sy.at[s, d, 1], r2.at[s, tx, tz, d]))
        parts = pl.ds(0, 2 if s == 0 else 1)
        for tx in range(2):
            plan.append(((tx, 0, 1), zo.at[s, parts], rz.at[s, tx, parts]))
        rows = pl.ds(0, 9 if s == 0 else 7)
        plan.append(((1, 0, 0), own.at[s, rows], par.at[s, rows]))
        copies = []
        for i, (to, src, dst) in enumerate(plan):
            copy = pltpu.make_async_remote_copy(
                src_ref=src,
                dst_ref=dst,
                send_sem=send_sem.at[s, i],
                recv_sem=recv_sem.at[s, i],
                device_id=device(*to),
                device_id_type=MESH,
            )
            copy.start()
            copies.append(copy)
        return copies

    edge_x = {1: cx == 3, -1: cx == 0}

    def along_x(two, a):
        if a == 0:
            return two[0]
        return jnp.where(edge_x[a], roll(two[1], 48 * a), roll(two[0], -16 * a))

    def along_z(value, beyond, c):
        if c == 0:
            return value
        return jnp.where(z == (15 if c == 1 else 0), beyond, roll(value, -c))

    def four(rows):
        p0, p1, y = rows
        return [p0, p1, jnp.where(lower, y, p0), jnp.where(lower, p1, y)]

    def twisted(p0, p1):
        return [roll(jnp.where(lower, p1, p0), 64), roll(jnp.where(lower, p0, p1), 64)]

    uses = {0: (0, 1), 1: (1, 2), -1: (0, 3)}

    def pair_weights():
        row = lax.broadcasted_iota(jnp.int32, (8, 128), 0)
        power = [jnp.left_shift(1, row + 8 * g).astype(F32) for g in range(2)]

        def total(value):
            return jnp.broadcast_to(jnp.sum(value, axis=0, keepdims=True), (8, 128))

        rows, thin_rows, thin_edges = [], [], []
        for dx in range(2):
            src = own.at[0] if dx == 0 else par.at[0]
            planes = [halves(src, q) for q in (7, 8)]
            p = [total(planes[0][v] * power[0] + planes[1][v] * power[1]) for v in range(2)]
            far = [
                total(ry[0, dx, d, 0] * jnp.where(lower, power[1 - d], power[d])) for d in range(2)
            ]
            y = jnp.where(lower, far[1], far[0])
            y = y + roll(jnp.where(lower, far[0], far[1]), 64)
            rows.append([p[0], p[1], y])
            thin = total(rz[0, dx, 1] * jnp.where(slot < 2, power[0], power[1]))
            thin_rows.append(thin + roll(thin, -4))
            thin = jnp.where(slot < 4, ryz[0, dx, 0], ryz[0, dx, 1])
            thin = total(thin * jnp.where((slot < 4) == lower, power[1], power[0]))
            thin_edges.append(thin + roll(thin, 64))
        mine = [value.astype(jnp.int32) for value in rows[0][:2]]
        mine_twisted = [value.astype(jnp.int32) for value in twisted(rows[0][0], rows[0][1])]
        for a in (-1, 0, 1):
            near = [along_x([rows[0][i], rows[1][i]], a) for i in range(3)]
            other, other_edge = along_x(thin_rows, a), along_x(thin_edges, a)
            beyond = [perm(other, group + 2 * v + swapped) for v in range(2)]
            beyond.append(perm(other_edge, group + jnp.where(lower, 14, 6) + swapped))
            for c in (-1, 0, 1):
                shifted = None
                for b in (-1, 0, 1):
                    offset = (a, b, c)
                    if offset >= (0, 0, 0):
                        number = 0 if offset == (0, 0, 0) else 1 + half_shell.index(offset)
                        two = mine if b == 0 else mine_twisted
                    else:
                        number = 1 + half_shell.index((-a, -b, -c))
                        if shifted is None:
                            shifted = four([along_z(near[i], beyond[i], c).astype(jnp.int32) for i in range(3)])
                        two = [shifted[i] for i in uses[b]]
                    for v in range(2):
                        listed = ((two[v] >> number) & 1) == 1
                        away[3 * a + c + 4, b + 1, v] = jnp.where(listed, F32(a), F32(FAR))

    def assemble(s):
        listed = [[lists_ref[s, m, d] for m in range(2)] for d in range(4)]

        def member(k, names):
            out = k == names[0]
            for name in names[1:]:
                out = out | (k == name)
            return out

        def first(k, d):
            return jnp.where(k == listed[d][1], 16, 0)

        both = listed[0] + listed[1]
        column = [cx * 4 + (lane >> 6) + 2 * v for v in range(2)]
        swap = [member(k, both) for k in column]
        back = [member(k, listed[3]) for k in column]
        moved = [member(k, listed[2]) | back[v] for v, k in enumerate(column)]
        place = [first(k, 2) + first(k, 3) + z for k in column]
        index = [
            [place[v] + jnp.where(back[v], 64, 0) for v in range(2)],
            [place[v] + jnp.where(back[v], 0, 64) for v in range(2)],
        ]
        k = cx * 4 + jnp.where(lower, 0, 3)
        swap_y = member(k, both)
        hit = [member(k, listed[2]), member(k, listed[3])]
        far_y = (hit[1] & lower) | (hit[0] & ~lower)
        self_y = (hit[0] & lower) | (hit[1] & ~lower)
        place_y = jnp.where(lower, first(k, 3) + 64, first(k, 2)) + z
        index_y = [place_y, place_y ^ 64]
        end = lane & 1
        k = cx * 4 + (lane >> 6) + 2 * (slot & 1)
        swap_o = member(k, both)
        hit_o = member(k, listed[3])
        moved_o = member(k, listed[2]) | hit_o
        index_o = ((slot >> 1) * 32) + first(k, 2) + first(k, 3) + end
        index_o = jnp.where(hit_o, (index_o ^ 64) + 12, index_o + 4)
        behind = slot < 4
        half = jnp.where(behind, 1, 0) ^ (lane >> 6)
        q_r = 2 * (slot & 1) + half
        k = cx * 4 + jnp.where(behind, 3, 0)
        swap_r = member(k, both)
        hit = [member(k, listed[2]), member(k, listed[3])]
        far_r = (hit[0] & behind) | (hit[1] & ~behind)
        self_r = (hit[1] & behind) | (hit[0] & ~behind)
        index_r = jnp.where(behind, q_r * 32 + first(k, 2) + 4, ((q_r * 32) ^ 64) + first(k, 3) + 12) + end
        index_s = cx * 16 + 4 * q_r + end + jnp.where(behind, 66, 0)

        yield None
        thin_rows, thin_edges = [], []
        merged = [
            jnp.where(behind, ryz[s, dx, 0], ryz[s, dx, 1]) for dx in range(2)
        ]
        ends = [rz[s, dx, 0] for dx in range(2)]
        for dx in range(2):
            value = jnp.where(moved_o, perm(merged[dx], index_o), ends[dx])
            thin_rows.append(jnp.where(swap_o, ends[1 - dx], value))
            beyond = jnp.where(behind, r2[s, dx, 1, 0], r2[s, dx, 1, 1])
            value = jnp.where(far_r, perm(beyond, index_r), merged[dx])
            value = jnp.where(self_r, perm(ends[dx], index_s), value)
            thin_edges.append(jnp.where(swap_r, merged[1 - dx], value))
        other = {a: along_x(thin_rows, a) for a in (-1, 0, 1)}
        other_edge = {a: along_x(thin_edges, a) for a in (-1, 0, 1)}

        near_list = [[ry[s, dx, d, 1] for d in range(2)] for dx in range(2)]
        far_list = [[r2[s, dx, 0, d] for d in range(2)] for dx in range(2)]

        def mix(two, q):
            return jnp.where(lower, two[q // 2], two[1 - q // 2])

        state = [None] * 7
        for q in range(4):
            plane = [halves(own, s, q), halves(par, s, q)]
            edge = []
            for dx in range(2):
                packed = [ry[s, dx, d, 2 + q // 2] for d in range(2)]
                if q % 2:
                    edge.append(roll(jnp.where(lower, packed[0], packed[1]), 64))
                else:
                    edge.append(jnp.where(lower, packed[1], packed[0]))
            odd = 32 * (q % 2)
            rows = []
            for dx in range(2):
                source = mix(near_list[dx], q)
                p = []
                for v in range(2):
                    value = jnp.where(moved[v], perm(source, index[q // 2][v] + odd), plane[dx][v])
                    p.append(jnp.where(swap[v], plane[1 - dx][v], value))
                y = jnp.where(far_y, perm(mix(far_list[dx], q), index_y[q // 2] + odd), edge[dx])
                y = jnp.where(self_y, jnp.where(lower, plane[dx][0], plane[dx][1]), y)
                rows.append([p[0], p[1], jnp.where(swap_y, edge[1 - dx], y)])
            state[q] = rows[0][:2]
            from_edge = cx * 16 + 2 * (q // 2) + swapped + jnp.where(lower, 64 * (q % 2) + 8, 64 * (1 - q % 2))
            for a in (-1, 0, 1):
                near = [along_x([rows[0][i], rows[1][i]], a) for i in range(3)]
                beyond = [perm(other[a], group + (4 * q + 2 * v) + swapped) for v in range(2)]
                beyond.append(perm(other_edge[a], from_edge))
                for c in (-1, 0, 1):
                    values = [along_z(near[i], beyond[i], c) for i in range(3)]
                    ac = 3 * a + c + 4
                    if q == 2 and c:
                        values = [value + F32(c) for value in values]
                    if q == 3:
                        values = [value.astype(jnp.int32) for value in values]
                    values = four(values)
                    if q == 0:
                        for b in (-1, 0, 1):
                            for v in range(2):
                                near_x[ac, b + 1, v] = values[uses[b][v]] + away[ac, b + 1, v]
                    else:
                        for i in range(4):
                            if q == 3:
                                near_type[ac, i] = values[i]
                            else:
                                near_yz[q - 1, ac, i] = values[i]
        speeds = [[ry[s, 0, d, 4] for d in range(2)], None]
        for q in range(3):
            mine, theirs = halves(own, s, 4 + q), halves(par, s, 4 + q)
            state[4 + q] = []
            for v in range(2):
                value = perm(mix(speeds[0], q), index[q // 2][v] + 32 * (q % 2))
                value = jnp.where(moved[v], value, mine[v])
                state[4 + q].append(jnp.where(swap[v], theirs[v], value))
        yield state

    def forces(state, table):
        beads = [state[q] + twisted(state[q][0], state[q][1]) for q in range(4)]
        kinds = [value.astype(jnp.int32) for value in beads[3]]
        base = [(value & 7) * 16 for value in kinds]
        lift = [(value >> 3) << 4 for value in kinds]
        beads_y = {b: [value - F32(b) if b else value for value in beads[1]] for b in (-1, 0, 1)}

        def add(ac, sums):
            sums = list(sums)
            for b in (-1, 0, 1):
                for v in range(2):
                    i = v if b == 0 else 2 + v
                    at = uses[b][v]
                    for j in range(8):
                        def bead(ref, *lead):
                            return jnp.broadcast_to(ref[(*lead, slice(j, j + 1), slice(None))], (8, 128))

                        d = [
                            beads[0][i] - bead(near_x, ac, b + 1, v),
                            beads_y[b][i] - bead(near_yz, 0, ac, at),
                            beads[2][i] - bead(near_yz, 1, ac, at),
                        ]
                        apart = d[0] * d[0] + d[1] * d[1] + (d[2] * d[2] + SOFT)
                        u = pl.reciprocal(apart, approx=True)
                        reach = jnp.maximum(u - NEAR, 0.0)
                        index = base[i] + bead(near_type, ac, at)
                        strength = lax.shift_right_logical(perm(table, index) << lift[i], 16).astype(F32)
                        w = (u * u - 1.0) * (reach * reach) * strength
                        for q in range(3):
                            sums[q * 4 + i] = sums[q * 4 + i] + w * d[q]
            return tuple(sums)

        zero = jnp.zeros((8, 128), F32)
        sums = lax.fori_loop(0, 9, add, (zero,) * 12, unroll=9)
        force = []
        for q in range(3):
            p0, p1, t1, t2 = sums[4 * q : 4 * q + 4]
            force.append([
                (p0 + roll(jnp.where(lower, t1, t2), 64)) * UNIT,
                (p1 + roll(jnp.where(lower, t2, t1), 64)) * UNIT,
            ])
        return force

    pack(0)
    pl.semaphore_wait(barrier, len(partners))
    pending = []
    for s in range(STEPS):
        copies = send(s)
        pending += copies
        assembly = assemble(s)
        next(assembly)
        if s == 0:
            table = strengths()
        for copy in copies:
            copy.wait_recv()
        if s == 0:
            pair_weights()
        state = next(assembly)
        force = forces(state, table)
        for q in range(3):
            speed, place = [], []
            for v in range(2):
                speed.append(state[4 + q][v] + STEP_TIME * force[q][v])
                place.append(state[q][v] + STEP_TIME * speed[v])
            if s == STEPS - 1:
                for v in range(2):
                    at = slice(v * 128, v * 128 + 128)
                    result[q, :, at] = place[v]
                    result[3 + q, :, at] = speed[v]
            else:
                for v in range(2):
                    at = slice(v * 128, v * 128 + 128)
                    own[s + 1, q, :, at] = place[v]
                    own[s + 1, 4 + q, :, at] = speed[v]
        if s < STEPS - 1:
            for v in range(2):
                own[s + 1, 3, :, v * 128 : v * 128 + 128] = state[3][v]
            pack(s + 1)
    out = pltpu.make_async_copy(result, result_hbm, out_sem)
    out.start()
    for copy in pending:
        copy.wait_send()
    out.wait()


def finish(result_hbm, pos_hbm, vel_hbm, result, pos, vel, sem):
    loads = [
        pltpu.make_async_copy(result_hbm.at[pl.ds(3 * i, 3)], result.at[pl.ds(3 * i, 3)], sem.at[i]) for i in range(2)
    ]
    for load in loads:
        load.start()
    stores = []
    for i, (rows, out) in enumerate(((pos, pos_hbm), (vel, vel_hbm))):
        loads[i].wait()
        for q in range(3):
            value = halves(result, 3 * i + q)
            for part in range(8):
                for v in range(2):
                    k = (part % 4) * 4 + v * 2 + part // 4
                    piece = roll(value[v], -16 * part) if part else value[v]
                    rows[pl.ds(q * 128 + k, 8, stride=16), :] = piece[:, :16]
            at = pl.ds(128 * q, 128)
            store = pltpu.make_async_copy(rows.at[at], out.at[at], sem.at[2 + 3 * i + q])
            store.start()
            stores.append(store)
    for store in stores:
        store.wait()


def body(coords, velocity, bead_type, eps_table, pair_list, migration):
    hbm = pl.BlockSpec(memory_space=pltpu.HBM)

    def buffer(*shape, dtype=F32):
        return pltpu.VMEM(shape, dtype)

    result = pl.pallas_call(
        kernel,
        out_shape=jax.ShapeDtypeStruct((6, 8, 256), F32),
        in_specs=[hbm] * 6,
        out_specs=hbm,
        scratch_shapes=[
            buffer(384, 16),
            buffer(384, 16),
            buffer(128, 16, dtype=jnp.int32),
            buffer(256, 16, dtype=jnp.int32),
            buffer(16, 16),
            pltpu.SMEM((2, 2, 4), jnp.int32),
            buffer(2, 9, 8, 256),
            buffer(2, 9, 8, 256),
            buffer(2, 2, 5, 8, 128),
            buffer(2, 2, 8, 128),
            buffer(2, 2, 8, 128),
            buffer(2, 2, 2, 5, 8, 128),
            buffer(2, 2, 2, 8, 128),
            buffer(2, 2, 2, 8, 128),
            buffer(2, 2, 2, 2, 8, 128),
            buffer(9, 3, 2, 8, 128),
            buffer(2, 9, 4, 8, 128),
            buffer(9, 4, 8, 128, dtype=jnp.int32),
            buffer(9, 3, 2, 8, 128),
            buffer(6, 8, 256),
            pltpu.SemaphoreType.DMA,
            pltpu.SemaphoreType.DMA((6,)),
            pltpu.SemaphoreType.DMA((2, 19)),
            pltpu.SemaphoreType.DMA((2, 19)),
        ],
        compiler_params=pltpu.CompilerParams(
            collective_id=0, has_side_effects=True
        ),
    )(
        coords.reshape(384, 16),
        velocity.reshape(384, 16),
        bead_type.reshape(128, 16),
        eps_table,
        pair_list.reshape(224, 16),
        migration.transpose(0, 2, 1),
    )
    positions, velocities = pl.pallas_call(
        finish,
        out_shape=(jax.ShapeDtypeStruct((384, 16), F32),) * 2,
        in_specs=[hbm],
        out_specs=(hbm, hbm),
        scratch_shapes=[
            buffer(6, 8, 256),
            buffer(384, 16),
            buffer(384, 16),
            pltpu.SemaphoreType.DMA((8,)),
        ],
    )(result)
    return positions.reshape(coords.shape), velocities.reshape(velocity.shape)


def solution(mesh):
    placed = (
        P(None, None, "gx", "gy", "gz"),
        P(None, None, "gx", "gy", "gz"),
        P(None, "gx", "gy", "gz"),
        P(),
        P(None, "gx", "gy", "gz"),
        P(),
    )
    return jax.shard_map(
        body,
        mesh=mesh,
        in_specs=placed,
        out_specs=(P(None, None, "gx", "gy", "gz"), P(None, None, "gx", "gy", "gz")),
        check_vma=False,
    )
```

```python
import functools

import jax
import jax.numpy as jnp
from jax import lax
from jax.experimental import pallas as pl
from jax.experimental.pallas import tpu as pltpu
from jax.sharding import PartitionSpec as P

MESH = pl.DeviceIdType.MESH
F32 = jnp.float32
STEPS = 2
STEP_TIME = 0.02
SOFT = 0.3
NEAR = 1.0 / (2.25 + 0.3)
UNIT = ((2.25 + 0.3) / 2.25) ** 2 * 2.0 / 65535.0
FAR = 1.0e3
half_shell = [
    (a, b, c) for a in (-1, 0, 1) for b in (-1, 0, 1) for c in (-1, 0, 1) if (a, b, c) > (0, 0, 0)
]


def column_lane(k):
    cx, cy = k // 4, k % 4
    return cy // 2, (cy % 2) * 64 + cx * 16


def roll(x, count):
    return pltpu.roll(x, count % 128, 1)


def perm(x, index):
    return jnp.take_along_axis(x, index, axis=1, mode="promise_in_bounds")


def halves(ref, *lead):
    return [ref[(*lead, slice(None), slice(v * 128, v * 128 + 128))] for v in range(2)]


def kernel(
    coords_hbm, velocity_hbm, type_hbm, eps_hbm, pairs_hbm, lists_hbm,
    result_hbm,
    raw_c, raw_v, raw_t, raw_p, eps_ref, lists_ref,
    own, par, sy, zo, zy, ry, rz, ryz, r2,
    near_x, near_yz, near_type, away, result, out_sem,
    in_sem, send_sem, recv_sem,
):
    gx, gy, gz = lax.axis_index("gx"), lax.axis_index("gy"), lax.axis_index("gz")
    ring = lax.axis_size("gy")

    def device(tx, dy, tz):
        return (
            1 - gx if tx else gx,
            lax.rem(gy + (dy + ring), ring) if dy else gy,
            1 - gz if tz else gz,
        )

    partners = [
        (tx, dy, tz)
        for dy in (1, -1, 2, -2, 0)
        for tz in (0, 1)
        for tx in (0, 1)
        if (tx, dy, tz) != (0, 0, 0)
    ]
    loads = [
        pltpu.make_async_copy(coords_hbm, raw_c, in_sem.at[0]),
        pltpu.make_async_copy(velocity_hbm, raw_v, in_sem.at[1]),
        pltpu.make_async_copy(type_hbm, raw_t, in_sem.at[2]),
        pltpu.make_async_copy(pairs_hbm, raw_p.at[pl.ds(0, 224)], in_sem.at[3]),
        pltpu.make_async_copy(eps_hbm, eps_ref, in_sem.at[4]),
        pltpu.make_async_copy(lists_hbm, lists_ref, in_sem.at[5]),
    ]
    barrier = pltpu.get_barrier_semaphore()
    for partner in partners:
        pl.semaphore_signal(barrier, inc=1, device_id=device(*partner), device_id_type=MESH)
    for load in loads:
        load.start()

    raw_p[pl.ds(224, 32), :] = jnp.zeros((32, 16), jnp.int32)
    for load in loads:
        load.wait()
    lane = lax.broadcasted_iota(jnp.int32, (8, 128), 1)
    z = lane & 15
    group = lane & ~15
    cx = (lane >> 4) & 3
    lower = lane < 64
    swapped = jnp.where(z == 15, 0, 1)
    slot = (lane >> 1) & 7

    tables = []
    tiled = [jnp.concatenate([eps_ref[r : r + 1, :]] * 8, axis=1) for r in range(16)]
    tiled = [jnp.broadcast_to(row, (8, 128)) for row in tiled]
    for h in range(2):
        direct = jnp.zeros((8, 128), F32)
        transposed = jnp.zeros((8, 128), F32)
        for r in range(8):
            direct = jnp.where((lane >> 4) == r, tiled[8 * h + r], direct)
        for c in range(16):
            transposed = jnp.where(z == c, perm(tiled[c], (lane >> 4) + 8 * h), transposed)
        tables.append((direct + transposed) * (65535.0 / 4.0) + 0.5)

    high, rest = [value.astype(jnp.int32) for value in tables]
    table = (high << 16) | rest

    sources = [(raw_c, 0), (raw_c, 1), (raw_c, 2), (raw_t, 0), (raw_v, 0), (raw_v, 1), (raw_v, 2), (raw_p, 0), (raw_p, 1)]
    for q, (raw, block) in enumerate(sources):
        for v in range(2):
            pieces = []
            for part in range(8):
                k = (part % 4) * 4 + v * 2 + part // 4
                pieces.append(raw[pl.ds(block * 128 + k, 8, stride=16), :])
            own[0, q, :, v * 128 : v * 128 + 128] = jnp.concatenate(pieces, axis=1).astype(F32)

    def pack(s):
        state = [halves(own, s, q) for q in range(9 if s == 0 else 7)]
        ends = group + 15 * (lane & 1)
        for d in range(2):

            def pair(first, second):
                if d == 0:
                    return jnp.where(lower, roll(state[second][1], 64), state[first][1])
                return jnp.where(lower, state[first][0], roll(state[second][0], 64))

            a, b = pair(0, 1), pair(2, 3)
            listed = []
            for rows in ((0, 1, 2, 3), (4, 5, 6)):
                out = jnp.zeros((8, 128), F32)
                for m in range(2):
                    k = lists_ref[s, m, 2 + d]
                    in_second = (k & 3) >= 2
                    index = (k & 1) * 64 + (k >> 2) * 16 + z
                    for i, q in enumerate(rows):
                        value = jnp.where(in_second, state[q][1], state[q][0])
                        out = jnp.where((lane >> 4) == (2 * i + m) ^ (4 * d), perm(value, index), out)
                listed.append(out)
            sy[s, d, 1] = listed[0]
            sy[s, d, 2] = a
            sy[s, d, 3] = b
            sy[s, d, 4] = listed[1]
            thin = jnp.zeros((8, 128), F32)
            slots = [a, b, listed[0]]
            if s == 0:
                p = pair(7, 8)
                sy[s, d, 0] = p
                slots.append(p)
            for i, value in enumerate(slots):
                thin = jnp.where(slot == i + 4 * d, perm(value, ends), thin)
            zy[s, d] = thin
        for part, rows in enumerate(((0, 1, 2, 3), (7, 8))[: 2 if s == 0 else 1]):
            thin = jnp.zeros((8, 128), F32)
            for i, q in enumerate(rows):
                for v in range(2):
                    thin = jnp.where(slot == 2 * i + v, perm(state[q][v], ends), thin)
            zo[s, part] = thin

    def send(s):
        first = 0 if s == 0 else 1
        plan = []
        wide, narrow = pl.ds(first, 5 - first), pl.ds(first, 4 - first)
        for d, dy in ((0, 1), (1, -1)):
            plan.append(((1, dy, 0), sy.at[s, d, narrow], ry.at[s, 1, d, narrow]))
        for d, dy in ((0, 1), (1, -1)):
            plan.append(((0, dy, 0), sy.at[s, d, wide], ry.at[s, 0, d, wide]))
        for d, dy in ((0, 1), (1, -1)):
            for tx in range(2):
                plan.append(((tx, dy, 1), zy.at[s, d], ryz.at[s, tx, d]))
        for d, dy in ((0, 2), (1, -2)):
            for tx in range(2):
                for tz in range(2):
                    plan.append(((tx, dy, tz), zy.at[s, d] if tz else sy.at[s, d, 1], r2.at[s, tx, tz, d]))
        parts = pl.ds(0, 2 if s == 0 else 1)
        for tx in range(2):
            plan.append(((tx, 0, 1), zo.at[s, parts], rz.at[s, tx, parts]))
        rows = pl.ds(0, 9 if s == 0 else 7)
        plan.append(((1, 0, 0), own.at[s, rows], par.at[s, rows]))
        copies = []
        for i, (to, src, dst) in enumerate(plan):
            copy = pltpu.make_async_remote_copy(
                src_ref=src,
                dst_ref=dst,
                send_sem=send_sem.at[s, i],
                recv_sem=recv_sem.at[s, i],
                device_id=device(*to),
                device_id_type=MESH,
            )
            copy.start()
            copies.append(copy)
        return copies

    edge_x = {1: cx == 3, -1: cx == 0}

    def along_x(two, a):
        if a == 0:
            return two[0]
        return jnp.where(edge_x[a], roll(two[1], 48 * a), roll(two[0], -16 * a))

    def along_z(value, beyond, c):
        if c == 0:
            return value
        return jnp.where(z == (15 if c == 1 else 0), beyond, roll(value, -c))

    def four(rows):
        p0, p1, y = rows
        return [p0, p1, jnp.where(lower, y, p0), jnp.where(lower, p1, y)]

    def twisted(p0, p1):
        return [roll(jnp.where(lower, p1, p0), 64), roll(jnp.where(lower, p0, p1), 64)]

    uses = {0: (0, 1), 1: (1, 2), -1: (0, 3)}

    def pair_weights():
        row = lax.broadcasted_iota(jnp.int32, (8, 128), 0)
        power = [jnp.left_shift(1, row + 8 * g).astype(F32) for g in range(2)]

        def total(value):
            return jnp.broadcast_to(jnp.sum(value, axis=0, keepdims=True), (8, 128))

        rows, thin_rows, thin_edges = [], [], []
        for dx in range(2):
            src = own.at[0] if dx == 0 else par.at[0]
            planes = [halves(src, q) for q in (7, 8)]
            p = [total(planes[0][v] * power[0] + planes[1][v] * power[1]) for v in range(2)]
            far = [
                total(ry[0, dx, d, 0] * jnp.where(lower, power[1 - d], power[d])) for d in range(2)
            ]
            y = jnp.where(lower, far[1], far[0])
            y = y + roll(jnp.where(lower, far[0], far[1]), 64)
            rows.append([p[0], p[1], y])
            thin = total(rz[0, dx, 1] * jnp.where(slot < 2, power[0], power[1]))
            thin_rows.append(thin + roll(thin, -4))
            thin = jnp.where(slot < 4, ryz[0, dx, 0], ryz[0, dx, 1])
            thin = total(thin * jnp.where((slot < 4) == lower, power[1], power[0]))
            thin_edges.append(thin + roll(thin, 64))
        mine = [value.astype(jnp.int32) for value in rows[0][:2]]
        mine_twisted = [value.astype(jnp.int32) for value in twisted(rows[0][0], rows[0][1])]
        for a in (-1, 0, 1):
            near = [along_x([rows[0][i], rows[1][i]], a) for i in range(3)]
            other, other_edge = along_x(thin_rows, a), along_x(thin_edges, a)
            beyond = [perm(other, group + 2 * v + swapped) for v in range(2)]
            beyond.append(perm(other_edge, group + jnp.where(lower, 14, 6) + swapped))
            for c in (-1, 0, 1):
                shifted = None
                for b in (-1, 0, 1):
                    offset = (a, b, c)
                    if offset >= (0, 0, 0):
                        number = 0 if offset == (0, 0, 0) else 1 + half_shell.index(offset)
                        two = mine if b == 0 else mine_twisted
                    else:
                        number = 1 + half_shell.index((-a, -b, -c))
                        if shifted is None:
                            shifted = four([along_z(near[i], beyond[i], c).astype(jnp.int32) for i in range(3)])
                        two = [shifted[i] for i in uses[b]]
                    for v in range(2):
                        listed = ((two[v] >> number) & 1) == 1
                        away[3 * a + c + 4, b + 1, v] = jnp.where(listed, F32(a), F32(FAR))

    def assemble(s):
        listed = [[lists_ref[s, m, d] for m in range(2)] for d in range(4)]

        def member(k, names):
            out = k == names[0]
            for name in names[1:]:
                out = out | (k == name)
            return out

        def first(k, d):
            return jnp.where(k == listed[d][1], 16, 0)

        both = listed[0] + listed[1]
        column = [cx * 4 + (lane >> 6) + 2 * v for v in range(2)]
        swap = [member(k, both) for k in column]
        back = [member(k, listed[3]) for k in column]
        moved = [member(k, listed[2]) | back[v] for v, k in enumerate(column)]
        place = [first(k, 2) + first(k, 3) + z for k in column]
        index = [
            [place[v] + jnp.where(back[v], 64, 0) for v in range(2)],
            [place[v] + jnp.where(back[v], 0, 64) for v in range(2)],
        ]
        k = cx * 4 + jnp.where(lower, 0, 3)
        swap_y = member(k, both)
        hit = [member(k, listed[2]), member(k, listed[3])]
        far_y = (hit[1] & lower) | (hit[0] & ~lower)
        self_y = (hit[0] & lower) | (hit[1] & ~lower)
        place_y = jnp.where(lower, first(k, 3) + 64, first(k, 2)) + z
        index_y = [place_y, place_y ^ 64]
        end = lane & 1
        k = cx * 4 + (lane >> 6) + 2 * (slot & 1)
        swap_o = member(k, both)
        hit_o = member(k, listed[3])
        moved_o = member(k, listed[2]) | hit_o
        index_o = ((slot >> 1) * 32) + first(k, 2) + first(k, 3) + end
        index_o = jnp.where(hit_o, (index_o ^ 64) + 12, index_o + 4)
        behind = slot < 4
        half = jnp.where(behind, 1, 0) ^ (lane >> 6)
        q_r = 2 * (slot & 1) + half
        k = cx * 4 + jnp.where(behind, 3, 0)
        swap_r = member(k, both)
        hit = [member(k, listed[2]), member(k, listed[3])]
        far_r = (hit[0] & behind) | (hit[1] & ~behind)
        self_r = (hit[1] & behind) | (hit[0] & ~behind)
        index_r = jnp.where(behind, q_r * 32 + first(k, 2) + 4, ((q_r * 32) ^ 64) + first(k, 3) + 12) + end
        index_s = cx * 16 + 4 * q_r + end + jnp.where(behind, 66, 0)

        thin_rows, thin_edges = [], []
        merged = [
            jnp.where(behind, ryz[s, dx, 0], ryz[s, dx, 1]) for dx in range(2)
        ]
        ends = [rz[s, dx, 0] for dx in range(2)]
        for dx in range(2):
            value = jnp.where(moved_o, perm(merged[dx], index_o), ends[dx])
            thin_rows.append(jnp.where(swap_o, ends[1 - dx], value))
            beyond = jnp.where(behind, r2[s, dx, 1, 0], r2[s, dx, 1, 1])
            value = jnp.where(far_r, perm(beyond, index_r), merged[dx])
            value = jnp.where(self_r, perm(ends[dx], index_s), value)
            thin_edges.append(jnp.where(swap_r, merged[1 - dx], value))
        other = {a: along_x(thin_rows, a) for a in (-1, 0, 1)}
        other_edge = {a: along_x(thin_edges, a) for a in (-1, 0, 1)}

        near_list = [[ry[s, dx, d, 1] for d in range(2)] for dx in range(2)]
        far_list = [[r2[s, dx, 0, d] for d in range(2)] for dx in range(2)]

        def mix(two, q):
            return jnp.where(lower, two[q // 2], two[1 - q // 2])

        state = [None] * 7
        for q in range(4):
            plane = [halves(own, s, q), halves(par, s, q)]
            edge = []
            for dx in range(2):
                packed = [ry[s, dx, d, 2 + q // 2] for d in range(2)]
                if q % 2:
                    edge.append(roll(jnp.where(lower, packed[0], packed[1]), 64))
                else:
                    edge.append(jnp.where(lower, packed[1], packed[0]))
            odd = 32 * (q % 2)
            rows = []
            for dx in range(2):
                source = mix(near_list[dx], q)
                p = []
                for v in range(2):
                    value = jnp.where(moved[v], perm(source, index[q // 2][v] + odd), plane[dx][v])
                    p.append(jnp.where(swap[v], plane[1 - dx][v], value))
                y = jnp.where(far_y, perm(mix(far_list[dx], q), index_y[q // 2] + odd), edge[dx])
                y = jnp.where(self_y, jnp.where(lower, plane[dx][0], plane[dx][1]), y)
                rows.append([p[0], p[1], jnp.where(swap_y, edge[1 - dx], y)])
            state[q] = rows[0][:2]
            from_edge = cx * 16 + 2 * (q // 2) + swapped + jnp.where(lower, 64 * (q % 2) + 8, 64 * (1 - q % 2))
            for a in (-1, 0, 1):
                near = [along_x([rows[0][i], rows[1][i]], a) for i in range(3)]
                beyond = [perm(other[a], group + (4 * q + 2 * v) + swapped) for v in range(2)]
                beyond.append(perm(other_edge[a], from_edge))
                for c in (-1, 0, 1):
                    values = [along_z(near[i], beyond[i], c) for i in range(3)]
                    ac = 3 * a + c + 4
                    if q == 2 and c:
                        values = [value + F32(c) for value in values]
                    if q == 3:
                        values = [value.astype(jnp.int32) for value in values]
                    values = four(values)
                    if q == 0:
                        for b in (-1, 0, 1):
                            for v in range(2):
                                near_x[ac, b + 1, v] = values[uses[b][v]] + away[ac, b + 1, v]
                    else:
                        for i in range(4):
                            if q == 3:
                                near_type[ac, i] = values[i]
                            else:
                                near_yz[q - 1, ac, i] = values[i]
        speeds = [[ry[s, 0, d, 4] for d in range(2)], None]
        for q in range(3):
            mine, theirs = halves(own, s, 4 + q), halves(par, s, 4 + q)
            state[4 + q] = []
            for v in range(2):
                value = perm(mix(speeds[0], q), index[q // 2][v] + 32 * (q % 2))
                value = jnp.where(moved[v], value, mine[v])
                state[4 + q].append(jnp.where(swap[v], theirs[v], value))
        return state

    def forces(state):
        beads = [state[q] + twisted(state[q][0], state[q][1]) for q in range(4)]
        kinds = [value.astype(jnp.int32) for value in beads[3]]
        base = [(value & 7) * 16 for value in kinds]
        lift = [(value >> 3) << 4 for value in kinds]
        beads_y = {b: [value - F32(b) if b else value for value in beads[1]] for b in (-1, 0, 1)}

        def add(ac, sums):
            sums = list(sums)
            for b in (-1, 0, 1):
                for v in range(2):
                    i = v if b == 0 else 2 + v
                    at = uses[b][v]
                    for j in range(8):
                        def bead(ref, *lead):
                            return jnp.broadcast_to(ref[(*lead, slice(j, j + 1), slice(None))], (8, 128))

                        d = [
                            beads[0][i] - bead(near_x, ac, b + 1, v),
                            beads_y[b][i] - bead(near_yz, 0, ac, at),
                            beads[2][i] - bead(near_yz, 1, ac, at),
                        ]
                        apart = d[0] * d[0] + d[1] * d[1] + (d[2] * d[2] + SOFT)
                        u = pl.reciprocal(apart, approx=True)
                        reach = jnp.maximum(u - NEAR, 0.0)
                        index = base[i] + bead(near_type, ac, at)
                        strength = lax.shift_right_logical(perm(table, index) << lift[i], 16).astype(F32)
                        w = (u * u - 1.0) * (reach * reach) * strength
                        for q in range(3):
                            sums[q * 4 + i] = sums[q * 4 + i] + w * d[q]
            return tuple(sums)

        zero = jnp.zeros((8, 128), F32)
        sums = lax.fori_loop(0, 9, add, (zero,) * 12, unroll=9)
        force = []
        for q in range(3):
            p0, p1, t1, t2 = sums[4 * q : 4 * q + 4]
            force.append([
                (p0 + roll(jnp.where(lower, t1, t2), 64)) * UNIT,
                (p1 + roll(jnp.where(lower, t2, t1), 64)) * UNIT,
            ])
        return force

    pack(0)
    pl.semaphore_wait(barrier, len(partners))
    pending = []
    for s in range(STEPS):
        copies = send(s)
        pending += copies
        for copy in copies:
            copy.wait_recv()
        if s == 0:
            pair_weights()
        state = assemble(s)
        force = forces(state)
        for q in range(3):
            speed, place = [], []
            for v in range(2):
                speed.append(state[4 + q][v] + STEP_TIME * force[q][v])
                place.append(state[q][v] + STEP_TIME * speed[v])
            if s == STEPS - 1:
                for v in range(2):
                    at = slice(v * 128, v * 128 + 128)
                    result[q, :, at] = place[v]
                    result[3 + q, :, at] = speed[v]
            else:
                for v in range(2):
                    at = slice(v * 128, v * 128 + 128)
                    own[s + 1, q, :, at] = place[v]
                    own[s + 1, 4 + q, :, at] = speed[v]
        if s < STEPS - 1:
            for v in range(2):
                own[s + 1, 3, :, v * 128 : v * 128 + 128] = state[3][v]
            pack(s + 1)
    out = pltpu.make_async_copy(result, result_hbm, out_sem)
    out.start()
    for copy in pending:
        copy.wait_send()
    out.wait()


def finish(result_hbm, pos_hbm, vel_hbm, result, pos, vel, sem):
    load = pltpu.make_async_copy(result_hbm, result, sem.at[0])
    load.start()
    load.wait()
    stores = []
    for i, (rows, out) in enumerate(((pos, pos_hbm), (vel, vel_hbm))):
        for q in range(3):
            value = halves(result, 3 * i + q)
            for part in range(8):
                for v in range(2):
                    k = (part % 4) * 4 + v * 2 + part // 4
                    piece = roll(value[v], -16 * part) if part else value[v]
                    rows[pl.ds(q * 128 + k, 8, stride=16), :] = piece[:, :16]
        stores.append(pltpu.make_async_copy(rows, out, sem.at[1 + i]))
        stores[i].start()
    for store in stores:
        store.wait()


def body(coords, velocity, bead_type, eps_table, pair_list, migration):
    hbm = pl.BlockSpec(memory_space=pltpu.HBM)

    def buffer(*shape, dtype=F32):
        return pltpu.VMEM(shape, dtype)

    result = pl.pallas_call(
        kernel,
        out_shape=jax.ShapeDtypeStruct((6, 8, 256), F32),
        in_specs=[hbm] * 6,
        out_specs=hbm,
        scratch_shapes=[
            buffer(384, 16),
            buffer(384, 16),
            buffer(128, 16, dtype=jnp.int32),
            buffer(256, 16, dtype=jnp.int32),
            buffer(16, 16),
            pltpu.SMEM((2, 2, 4), jnp.int32),
            buffer(2, 9, 8, 256),
            buffer(2, 9, 8, 256),
            buffer(2, 2, 5, 8, 128),
            buffer(2, 2, 8, 128),
            buffer(2, 2, 8, 128),
            buffer(2, 2, 2, 5, 8, 128),
            buffer(2, 2, 2, 8, 128),
            buffer(2, 2, 2, 8, 128),
            buffer(2, 2, 2, 2, 8, 128),
            buffer(9, 3, 2, 8, 128),
            buffer(2, 9, 4, 8, 128),
            buffer(9, 4, 8, 128, dtype=jnp.int32),
            buffer(9, 3, 2, 8, 128),
            buffer(6, 8, 256),
            pltpu.SemaphoreType.DMA,
            pltpu.SemaphoreType.DMA((6,)),
            pltpu.SemaphoreType.DMA((2, 19)),
            pltpu.SemaphoreType.DMA((2, 19)),
        ],
        compiler_params=pltpu.CompilerParams(
            collective_id=0, has_side_effects=True
        ),
    )(
        coords.reshape(384, 16),
        velocity.reshape(384, 16),
        bead_type.reshape(128, 16),
        eps_table,
        pair_list.reshape(224, 16),
        migration.transpose(0, 2, 1),
    )
    positions, velocities = pl.pallas_call(
        finish,
        out_shape=(jax.ShapeDtypeStruct((384, 16), F32),) * 2,
        in_specs=[hbm],
        out_specs=(hbm, hbm),
        scratch_shapes=[
            buffer(6, 8, 256),
            buffer(384, 16),
            buffer(384, 16),
            pltpu.SemaphoreType.DMA((3,)),
        ],
    )(result)
    return positions.reshape(coords.shape), velocities.reshape(velocity.shape)


def solution(mesh):
    placed = (
        P(None, None, "gx", "gy", "gz"),
        P(None, None, "gx", "gy", "gz"),
        P(None, "gx", "gy", "gz"),
        P(),
        P(None, "gx", "gy", "gz"),
        P(),
    )
    return jax.shard_map(
        body,
        mesh=mesh,
        in_specs=placed,
        out_specs=(P(None, None, "gx", "gy", "gz"), P(None, None, "gx", "gy", "gz")),
        check_vma=False,
    )
```
